256 devices in a mesh: tm: 64 (over z, x, core), tp: 4 (over y).
Axes of the slice: x: 4, y: 4, z: 8, core: 2. Of those that a mesh axis runs over, the one named last changes fastest.
Arguments:
- tokens: bfloat16 [24576, 1536], P('tm', 'tp')
- ln_gain: float32 [1536], replicated, may hold values from 0.1 to 1.9
- w_qkv: bfloat16 [1536, 3, 1536], P(None, None, 'tp')
- w_out: bfloat16 [1536, 1536], P(None, 'tp'), may hold values from -0.15625 to 0.15625
- frame_mask: int32 [24576], P('tm'), may hold values from 0 to 1, as said below
- out_grad: bfloat16 [24576, 1536], P('tm', 'tp')
Outputs:
- layer_out: bfloat16 [24576, 1536], P('tm', 'tp')
- tokens_grad: bfloat16 [24576, 1536], P('tm', 'tp')
- gain_grad: float32 [1536], replicated
- qkv_grad: float32 [1536, 3, 1536], P('tm', None, 'tp')
- out_weight_grad: float32 [1536, 1536], P('tm', 'tp')
The draws below stay inside these ranges and needn't reach their ends.
Inputs may be any that keep to these rules, and one draw needn't show every extreme that they name: `frame_mask`: each frame is 0 with probability one quarter, independently, and every frame from the recording's valid length on is 0; the valid length lies between 24320 and 24575.
All inputs are finite; a program needn't handle non-finite values.
Results may differ from the reference program's by a relative error of at most 0.014.
Values may be sent and summed in bfloat16 or wider, within the bound.
No kernel may reach another device: no remote copies, remote signals or barrier semaphores. Data moves between devices by JAX's collectives and lax.ppermute only.
A program may use at most 128 MiB of HBM per device.

```python
import jax
import jax.numpy as jnp
from jax import lax

D = 1536
HEADS = 24
HEAD = 64
WINDOW = 128
TOK_DEV = 384
TOKENS = 24576


def draw_tokens(key, part):
    key = jax.random.fold_in(key, 5)
    stream_one = jax.random.fold_in(key, 0)
    sample = jnp.clip(jax.random.normal(stream_one, (TOKENS, D), jnp.float32), -6.0, 6.0)
    return sample.astype(jnp.bfloat16)


def draw_w_qkv(key, part):
    key = jax.random.fold_in(key, 11)
    stream_one = jax.random.fold_in(key, 0)
    drawn_values = jnp.clip(jax.random.normal(stream_one, (D, 3, D), jnp.float32), -6.0, 6.0) * D ** (-0.5)
    return drawn_values.astype(jnp.bfloat16)


def draw_frame_mask(key, part):
    key = jax.random.fold_in(key, 3)
    stream_one, stream_two = jax.random.split(key, 2)
    valid_length = jax.random.randint(stream_one, (), TOKENS - TOK_DEV + WINDOW, TOKENS)
    kept = jax.random.randint(stream_two, (TOKENS,), 0, 4) != 0
    inside = jnp.arange(TOKENS, dtype=jnp.int32) < valid_length
    return (inside & kept).astype(jnp.int32)


def draw_out_grad(key, part):
    key = jax.random.fold_in(key, 7)
    stream_one = jax.random.fold_in(key, 0)
    rising = 1.0 + 2.0 * jnp.arange(TOKENS, dtype=jnp.float32)[:, None] / (TOKENS - 1)
    sample = jnp.clip(jax.random.normal(stream_one, (TOKENS, D), jnp.float32), -6.0, 6.0) * rising
    return sample.astype(jnp.bfloat16)


def levels(key, dims, pieces, least, high):
    factor_of, own = 1.0, jax.random.fold_in(key, 6)
    for dim, shards_of in pieces:
        heights = jnp.exp(jax.random.uniform(jax.random.fold_in(own, dim), (shards_of,), jnp.float32, least / len(pieces), high / len(pieces)))
        factor_of = factor_of * jnp.repeat(heights, dims[dim] // shards_of).reshape([-1 if axis == dim else 1 for axis in range(len(dims))])
    return factor_of


def normal_values(own_key, extent, scale, bound, cuts=(), kind=jnp.bfloat16):
    gain = levels(own_key, extent, cuts, -0.22, 0.18) if cuts else 1.0
    entries = jax.random.normal(own_key, extent, jnp.float32) * scale * gain
    return jnp.minimum(jnp.maximum(entries, -bound), bound).astype(kind)


def setup_inputs(seed: int = 0) -> dict:
    keys = jax.random.split(jax.random.key(seed), 7)
    return {
        "tokens": draw_tokens(jax.random.fold_in(keys[6], 71), 0),
        "ln_gain": jnp.clip(1.0 + 0.18 * jax.random.normal(keys[1], (D,), jnp.float32), 0.1, 1.9),
        "w_qkv": draw_w_qkv(jax.random.fold_in(keys[6], 71), 0),
        "w_out": normal_values(keys[3], (D, D), D ** -0.5, 0.15625, ((1, 4),)),
        "frame_mask": draw_frame_mask(jax.random.fold_in(keys[6], 71), 0),
        "out_grad": draw_out_grad(jax.random.fold_in(keys[6], 71), 0),
    }


EPSILON = 1e-05

def rounded(value):
    return lax.optimization_barrier(value.astype(jnp.bfloat16)).astype(jnp.float32)

def window_softmax(queries, key_heads, query_place, key_place, key_valid, scaling):
    scores = jnp.einsum('qhe,khe->hqk', queries.astype(jnp.float32), key_heads.astype(jnp.float32)) * scaling
    nearby = jnp.abs(query_place[:, None] - key_place[None, :]) <= WINDOW
    allowed = nearby & key_valid[None, :] | (query_place[:, None] == key_place[None, :])
    scores = jnp.where(allowed[None], scores, -1e+30)
    largest = lax.optimization_barrier(jnp.max(scores, axis=-1, keepdims=True))
    exponent = jnp.where(allowed[None], jnp.exp(scores - largest), 0.0)
    return exponent / lax.optimization_barrier(jnp.sum(exponent, axis=-1, keepdims=True))

def reference(tokens, ln_gain, w_qkv, w_out, frame_mask, out_grad):
    tokens_wide = tokens.astype(jnp.float32)
    average = lax.optimization_barrier(jnp.mean(tokens_wide, axis=-1, keepdims=True))
    centered = tokens_wide - average
    inverse_std = lax.rsqrt(lax.optimization_barrier(jnp.mean(centered * centered, axis=-1, keepdims=True)) + EPSILON)
    whitened = centered * inverse_std
    normed = (whitened * ln_gain).astype(jnp.bfloat16)
    projected = jnp.dot(normed, w_qkv.reshape(D, 3 * D), preferred_element_type=jnp.float32)
    projected = projected.astype(jnp.bfloat16).reshape(TOKENS, 3, HEADS, HEAD)
    queries = projected[:, 0]
    padding = ((WINDOW, WINDOW), (0, 0), (0, 0))
    key_pad = jnp.pad(projected[:, 1], padding)
    value_pad = jnp.pad(projected[:, 2], padding)
    valid_pad = jnp.pad(frame_mask > 0, (WINDOW, WINDOW))
    scaling = HEAD ** (-0.5)
    span = TOK_DEV + 2 * WINDOW
    block_count = TOKENS // TOK_DEV

    def block_inputs(block_index):
        anchor = block_index.astype(jnp.int32) * TOK_DEV
        query_block = lax.dynamic_slice_in_dim(queries, anchor, TOK_DEV, 0)
        key_block = lax.dynamic_slice_in_dim(key_pad, anchor, span, 0)
        value_block = lax.dynamic_slice_in_dim(value_pad, anchor, span, 0)
        valid_block = lax.dynamic_slice_in_dim(valid_pad, anchor, span, 0)
        query_place = anchor + jnp.arange(TOK_DEV, dtype=jnp.int32)
        key_place = anchor - WINDOW + jnp.arange(span, dtype=jnp.int32)
        probability = window_softmax(query_block, key_block, query_place, key_place, valid_block, scaling)
        return (anchor, query_block, key_block, value_block, probability)

    def forward_block(block_index):
        anchor, query_block, key_block, value_block, probability = block_inputs(block_index)
        attended_block = jnp.einsum('hqk,khe->qhe', rounded(probability), value_block.astype(jnp.float32))
        return attended_block.astype(jnp.bfloat16)
    attended = lax.map(forward_block, jnp.arange(block_count, dtype=jnp.int32)).reshape(TOKENS, D)
    keep_rows = frame_mask.astype(jnp.float32)[:, None]
    branch = jnp.dot(attended, w_out.T, preferred_element_type=jnp.float32)
    layer_out = (tokens_wide + keep_rows * branch).astype(jnp.bfloat16)
    gated_rows = (out_grad.astype(jnp.float32) * keep_rows).astype(jnp.bfloat16)
    out_weight_grad = jnp.dot(gated_rows.T, attended, preferred_element_type=jnp.float32)
    attended_grad = jnp.dot(gated_rows, w_out, preferred_element_type=jnp.float32)
    attended_grad = attended_grad.astype(jnp.bfloat16).reshape(TOKENS, HEADS, HEAD)

    def backward_block(block_index, running):
        query_grads, pair_pad = running
        anchor, query_block, key_block, value_block, probability = block_inputs(block_index)
        grad_block = lax.dynamic_slice_in_dim(attended_grad, anchor, TOK_DEV, 0).astype(jnp.float32)
        probability_grad = jnp.einsum('qhe,khe->hqk', grad_block, value_block.astype(jnp.float32))
        row_dots = lax.optimization_barrier(jnp.sum(probability * probability_grad, axis=-1, keepdims=True))
        score_grad = rounded(probability * (probability_grad - row_dots) * scaling)
        query_part = jnp.einsum('hqk,khe->qhe', score_grad, key_block.astype(jnp.float32)).astype(jnp.bfloat16)
        key_part = jnp.einsum('hqk,qhe->khe', score_grad, query_block.astype(jnp.float32))
        value_part = jnp.einsum('hqk,qhe->khe', rounded(probability), grad_block)
        previous = lax.dynamic_slice_in_dim(pair_pad, anchor, span, 0)
        pair_pad = lax.dynamic_update_slice_in_dim(pair_pad, previous + jnp.stack([key_part, value_part], axis=1), anchor, 0)
        query_grads = lax.dynamic_update_slice_in_dim(query_grads, query_part, anchor, 0)
        return (query_grads, pair_pad)
    start_state = (jnp.zeros((TOKENS, HEADS, HEAD), jnp.bfloat16), jnp.zeros((TOKENS + 2 * WINDOW, 2, HEADS, HEAD), jnp.float32))
    query_grads, pair_pad = lax.fori_loop(jnp.int32(0), jnp.int32(block_count), backward_block, start_state)
    pair_grads = pair_pad[WINDOW:WINDOW + TOKENS].astype(jnp.bfloat16).reshape(TOKENS, 2, D)
    projected_grad = jnp.concatenate([query_grads.reshape(TOKENS, 1, D), pair_grads], axis=1)
    flattened = projected_grad.reshape(TOKENS, 3 * D)
    qkv_grad = jnp.dot(normed.T, flattened, preferred_element_type=jnp.float32).reshape(D, 3, D)
    norm_grad = jnp.dot(flattened, w_qkv.reshape(D, 3 * D).T, preferred_element_type=jnp.float32)
    gain_grad = lax.optimization_barrier(jnp.sum(norm_grad * whitened, axis=0))
    unit_grad = norm_grad * ln_gain
    first_mean = lax.optimization_barrier(jnp.mean(unit_grad, axis=-1, keepdims=True))
    second_mean = lax.optimization_barrier(jnp.mean(unit_grad * whitened, axis=-1, keepdims=True))
    tokens_grad = out_grad.astype(jnp.float32) + (unit_grad - first_mean - whitened * second_mean) * inverse_std
    return (layer_out, tokens_grad.astype(jnp.bfloat16), gain_grad, qkv_grad, out_weight_grad)
```

```python
import jax
import jax.numpy as jnp
from jax import lax
from jax.experimental import pallas as pl
from jax.experimental.pallas import tpu as pltpu
from jax.sharding import Mesh, PartitionSpec as P

HEAD = 64
WINDOW = 128
EPSILON = 1e-05
LANES = 128
TM = ("z", "x", "core")
F32 = jnp.float32
BF16 = jnp.bfloat16


def shifted(value, axis, by):
    size = lax.axis_size(axis)
    return lax.ppermute(value, axis, [(i, (i + by) % size) for i in range(size)])


def swapped(value, axis, bit):
    size = lax.axis_size(axis)
    return lax.ppermute(value, axis, [(i, i ^ bit) for i in range(size)])


def to_next(value):
    size = lax.axis_size(TM)
    return lax.ppermute(value, TM, [(i, i + 1) for i in range(size - 1)])


def to_previous(value):
    size = lax.axis_size(TM)
    return lax.ppermute(value, TM, [(i + 1, i) for i in range(size - 1)])


def dot_nn(a, b):
    return lax.dot_general(a, b, (((1,), (0,)), ((), ())), preferred_element_type=F32)


def dot_nt(a, b):
    return lax.dot_general(a, b, (((1,), (1,)), ((), ())), preferred_element_type=F32)


def dot_tn(a, b):
    return lax.dot_general(a, b, (((0,), (0,)), ((), ())), preferred_element_type=F32)


def call(body, outs, args, smem=(), scratch=(), flops=0, moved=0, vmem=48):
    in_specs = [
        pl.BlockSpec(memory_space=pltpu.SMEM if k in smem else pltpu.VMEM) for k in range(len(args))
    ]
    return pl.pallas_call(
        body,
        out_shape=[jax.ShapeDtypeStruct(s, d) for s, d in outs],
        in_specs=in_specs,
        out_specs=[pl.BlockSpec(memory_space=pltpu.VMEM)] * len(outs),
        scratch_shapes=list(scratch),
        cost_estimate=pl.CostEstimate(flops=flops, bytes_accessed=moved, transcendentals=0),
        compiler_params=pltpu.CompilerParams(vmem_limit_bytes=vmem * 2**20),
    )(*args)


def block_of(place, step):
    return lax.rem(place[3] + step, 4)


def project_kernel(
    place, t0, t1, t2, t3, gain, weights, normed, q_out, k_out, v_out, kv_low, kv_high, stats
):
    parts = (t0, t1, t2, t3)
    width = 4 * t0.shape[1]
    wide = [t[...].astype(F32) for t in parts]
    average = sum(jnp.sum(t, axis=1, keepdims=True) for t in wide) / width
    centered = [t - average for t in wide]
    variance = sum(jnp.sum(t * t, axis=1, keepdims=True) for t in centered) / width
    inverse_std = lax.rsqrt(variance + EPSILON)
    lane = lax.broadcasted_iota(jnp.int32, stats.shape, 1)
    stats[...] = jnp.where(lane == 0, average, inverse_std)
    for step in range(4):
        block = block_of(place, step)
        normed[block] = (centered[step] * inverse_std * gain[block]).astype(BF16)
    rows = t0.shape[1]
    for kind, out in enumerate((q_out, k_out, v_out)):
        total = None
        for block in range(4):
            term = dot_nn(normed[block], weights[kind, rows * block : rows * (block + 1), :])
            total = term if total is None else total + term
        out[...] = total.astype(BF16)
        if kind > 0:
            columns = slice((kind - 1) * rows, kind * rows)
            kv_low[:, columns] = out[:WINDOW, :]
            kv_high[:, columns] = out[out.shape[0] - WINDOW :, :]


def attention_kernel(
    place, mask, q_in, k_in, v_in, kv_prev, kv_next, g0, g1, g2, g3, w_out,
    attended, q_grad, kv_grad, kv_low, kv_high, gated,
    k_ext, v_ext, k_cross, v_cross, upstream, cap, dk_ext, dv_ext,
):
    frames, width = q_in.shape
    span = 3 * WINDOW
    blocks = frames // WINDOW
    turned = []
    for block in range(blocks + 2):
        row = mask[:, block * WINDOW : (block + 1) * WINDOW]
        turned.append(jnp.transpose(jnp.broadcast_to(row, (WINDOW, WINDOW))))
    key_at = lax.broadcasted_iota(jnp.int32, (WINDOW, WINDOW), 0)
    query_at = lax.broadcasted_iota(jnp.int32, (WINDOW, WINDOW), 1)
    high, low = 3.0e38, -1e30
    for block in range(blocks):
        before = (key_at >= query_at) & (turned[block] > 0)
        inside = (key_at == query_at) | (turned[block + 1] > 0)
        after = (key_at <= query_at) & (turned[block + 2] > 0)
        for part, allowed in enumerate((before, inside, after)):
            cap[block, part * WINDOW : (part + 1) * WINDOW, :] = jnp.where(allowed, high, low)

    total = None
    for step, ref in enumerate((g0, g1, g2, g3)):
        block = block_of(place, step)
        for part in range(blocks):
            rows = slice(part * WINDOW, (part + 1) * WINDOW)
            keep = turned[part + 1]
            keep = jnp.concatenate([keep] * (width // WINDOW), axis=1)
            gated[block, rows, :] = (ref[rows, :].astype(F32) * keep).astype(BF16)
    for block in range(4):
        term = dot_nn(gated[block], w_out[width * block : width * (block + 1), :])
        total = term if total is None else total + term
    upstream[...] = total.astype(BF16)

    for ext, own, at in ((k_ext, k_in, 0), (v_ext, v_in, width)):
        ext[:WINDOW, :] = kv_prev[:, at : at + width]
        ext[WINDOW : WINDOW + frames, :] = own[...]
        ext[WINDOW + frames :, :] = kv_next[:, at : at + width]
    dk_ext[...] = jnp.zeros_like(dk_ext)
    dv_ext[...] = jnp.zeros_like(dv_ext)
    scaling = HEAD ** (-0.5)
    first = lax.broadcasted_iota(jnp.int32, (WINDOW, LANES), 1) < HEAD
    for pair in range(width // LANES):
        lanes = slice(pair * LANES, (pair + 1) * LANES)
        k_cross[...] = jnp.transpose(k_ext[:, lanes].astype(F32) * scaling).astype(BF16)
        v_cross[...] = jnp.transpose(v_ext[:, lanes].astype(F32)).astype(BF16)
        for block in range(blocks):
            rows = slice(block * WINDOW, (block + 1) * WINDOW)
            keys = slice(block * WINDOW, block * WINDOW + span)
            query = q_in[rows, lanes] * jnp.asarray(scaling, BF16)
            zero = jnp.zeros_like(query)
            query = jnp.concatenate(
                [jnp.where(first, query, zero), jnp.where(first, zero, query)], axis=0
            )
            grad = upstream[rows, lanes]
            grad = jnp.concatenate(
                [jnp.where(first, grad, zero), jnp.where(first, zero, grad)], axis=0
            )
            bound = cap[block]
            bound = jnp.concatenate([bound, bound], axis=1)
            scores = jnp.minimum(dot_nt(k_ext[keys, lanes], query), bound)
            largest = jnp.max(scores, axis=0, keepdims=True)
            exponent = jnp.exp(scores - largest)
            probability = exponent * (1.0 / jnp.sum(exponent, axis=0, keepdims=True))
            probability_low = probability.astype(BF16)
            probability_grad = dot_nt(v_ext[keys, lanes], grad)
            row_dots = jnp.sum(probability * probability_grad, axis=0, keepdims=True)
            score_grad = (probability * (probability_grad - row_dots)).astype(BF16)
            dv_ext[keys, lanes] += dot_nn(probability_low, grad)
            dk_ext[keys, lanes] += dot_nn(score_grad, query)
            for cross, factor, out in (
                (v_cross, probability_low, attended),
                (k_cross, score_grad, q_grad),
            ):
                both = dot_nn(cross[:, keys], factor)
                both = jnp.concatenate([both[:HEAD, :WINDOW], both[HEAD:, WINDOW:]], axis=0)
                out[rows, lanes] = jnp.transpose(both).astype(BF16)
    for ext, at in ((dk_ext, 0), (dv_ext, width)):
        columns = slice(at, at + width)
        kv_low[:, columns] = ext[:WINDOW, :].astype(BF16)
        kv_grad[:, columns] = ext[WINDOW : WINDOW + frames, :]
        kv_high[:, columns] = ext[WINDOW + frames :, :].astype(BF16)


def split_rows(place, block, held, send, keep):
    core = place[2]
    for group in range(8):
        for out, whose in ((send, 1 - core), (keep, core)):
            start = pl.multiple_of(48 * group + 24 * whose, 8)
            both = jnp.concatenate([held[0, pl.ds(start, 24), :], held[1, pl.ds(start, 24), :]], 0)
            out[group % 4, 2 * block + group // 4] = both.astype(BF16)


def first_weights_kernel(
    place, gated, attended, q_grad, normed, w_out, send, keep, b0, b1, b2, b3, held
):
    width = attended.shape[1]
    for block in range(4):
        held[0] = dot_tn(gated[block], attended[...])
        held[1] = dot_tn(normed[block], q_grad[...])
        split_rows(place, block, held, send, keep)
    for step, out in enumerate((b0, b1, b2, b3)):
        block = block_of(place, step)
        rows = w_out[pl.ds(pl.multiple_of(width * block, width), width), :]
        out[...] = dot_nt(attended[...], rows).astype(BF16)


def second_weights_kernel(
    place, kv_grad, from_prev, from_next, q_grad, normed, weights, t0, t1, t2, t3, stats, gain,
    send, keep, n0, n1, n2, n3, gain_part, held, k_grad, v_grad,
):
    frames, width = q_grad.shape
    for out, at in ((k_grad, 0), (v_grad, width)):
        columns = slice(at, at + width)
        out[:WINDOW, :] = (
            kv_grad[:WINDOW, columns] + from_prev[:, columns].astype(F32)
        ).astype(BF16)
        out[WINDOW : frames - WINDOW, :] = kv_grad[WINDOW : frames - WINDOW, columns].astype(BF16)
        out[frames - WINDOW :, :] = (
            kv_grad[frames - WINDOW :, columns] + from_next[:, columns].astype(F32)
        ).astype(BF16)
    for block in range(4):
        held[0] = dot_tn(normed[block], k_grad[...])
        held[1] = dot_tn(normed[block], v_grad[...])
        split_rows(place, block, held, send, keep)
    average, inverse_std = stats[:, 0:1], stats[:, 1:2]
    first_sum = second_sum = None
    for step, (tokens, out) in enumerate(((t0, n0), (t1, n1), (t2, n2), (t3, n3))):
        block = block_of(place, step)
        start = pl.multiple_of(width * block, width)
        total = None
        for kind, part in enumerate((q_grad, k_grad, v_grad)):
            term = dot_nt(part[...], weights[kind, pl.ds(start, width), :])
            total = term if total is None else total + term
        whitened = (tokens[...].astype(F32) - average) * inverse_std
        if step == 0:
            out[...] = total
        else:
            out[:frames, :] = total.astype(BF16)
        gain_part[block] = jnp.sum(total * whitened, axis=0, keepdims=True)
        unit = total * gain[block]
        first = jnp.sum(unit, axis=1, keepdims=True)
        second = jnp.sum(unit * whitened, axis=1, keepdims=True)
        first_sum = first if first_sum is None else first_sum + first
        second_sum = second if second_sum is None else second_sum + second
    lane = lax.broadcasted_iota(jnp.int32, (frames, LANES), 1)
    sums = jnp.transpose(jnp.where(lane == 0, first_sum, jnp.where(lane == 1, second_sum, 0.0)))
    sums = sums[:8, :]
    head = sums.astype(BF16)
    rest = (sums - head.astype(F32)).astype(BF16)
    tail = jnp.concatenate([head.astype(F32), rest.astype(F32)], axis=0)
    for out in (n1, n2, n3):
        out[frames:, :] = tail.astype(BF16)
    gain_part[4] = sums[0:1, :]
    gain_part[5] = sums[1:2, :]


def tokens_kernel(gain_own, tokens, out_grad, stats, sums, own, r1, r2, r3, out):
    frames = tokens.shape[0]
    width = 4 * tokens.shape[1]
    average, inverse_std = stats[:, 0:1], stats[:, 1:2]
    total = own[...]
    rows = jnp.concatenate([sums[4], sums[5], jnp.zeros((6, frames), F32)], axis=0)
    for part in (r1, r2, r3):
        total = total + part[:frames, :].astype(F32)
        tail = part[frames:, :].astype(F32)
        rows = rows + tail[:8, :] + tail[8:, :]
    rows = jnp.concatenate([rows, jnp.zeros((LANES - 8, frames), F32)], axis=0) / width
    turned = jnp.transpose(rows)
    first_mean, second_mean = turned[:, 0:1], turned[:, 1:2]
    whitened = (tokens[...].astype(F32) - average) * inverse_std
    unit = total * gain_own[...]
    moved = (unit - first_mean - whitened * second_mean) * inverse_std
    out[...] = (out_grad[...].astype(F32) + moved).astype(BF16)


def core_sum_kernel(place, keep, received, own, p1, p2, p3):
    for step, out in enumerate((own, p1, p2, p3)):
        which = lax.rem(place[1] + step, 4)
        out[...] = (keep[which].astype(F32) + received[which].astype(F32)).astype(out.dtype)


def x_sum_kernel(place, own, r1, r2, r3, *outs):
    for step, out in enumerate(outs):
        which = lax.rem(place[0] + step, 8)
        total = own[which] + r1[which].astype(F32)
        total = total + r2[which].astype(F32) + r3[which].astype(F32)
        out[...] = total.astype(out.dtype)


def z_sum_kernel(own, *refs):
    parts, (upper, lower) = refs[:-2], refs[-2:]
    total = own[...]
    for part in parts:
        total = total + part[...].astype(F32)
    upper[...] = total[:24, :]
    lower[...] = total[24:, :]


def scatter_sum(place, send, keep):
    shape = send.shape
    received = swapped(send, "core", 1)
    own, *pieces = call(
        core_sum_kernel,
        [(shape[1:], F32)] + [(shape[1:], BF16)] * 3,
        (place, keep, received),
        smem=(0,),
        moved=6 * 2**20,
    )
    received = [shifted(piece, "x", by + 1) for by, piece in enumerate(pieces)]
    own, *pieces = call(
        x_sum_kernel,
        [(shape[2:], F32)] + [(shape[2:], BF16)] * 7,
        (place, own, *received),
        smem=(0,),
        moved=3 * 2**20,
    )
    received = [shifted(piece, "z", by + 1) for by, piece in enumerate(pieces)]
    return call(
        z_sum_kernel, [((24, shape[3]), F32)] * 2, (own, *received), moved=2**20
    )


def per_device(tokens, ln_gain, w_qkv, w_out, frame_mask, out_grad):
    frames, width = tokens.shape
    place = jnp.stack([lax.axis_index(a) for a in ("z", "x", "core", "tp")]).astype(jnp.int32)
    token_parts = [tokens] + [shifted(tokens, "tp", -step) for step in (1, 2, 3)]
    mask_before = to_next(frame_mask[frames - WINDOW :])
    mask_after = to_previous(frame_mask[:WINDOW])
    grad_parts = [out_grad] + [shifted(out_grad, "tp", -step) for step in (1, 2, 3)]
    mask_wide = jnp.concatenate([mask_before, frame_mask, mask_after]).astype(F32)[None, :]
    gain = ln_gain.reshape(4, 1, width)
    weights = jnp.transpose(w_qkv, (1, 0, 2))

    sheet, wide_sheet = ((frames, width), BF16), ((4, frames, width), BF16)
    edge = ((WINDOW, 2 * width), BF16)
    square = frames * width * width * 2
    normed, q_own, k_own, v_own, kv_low, kv_high, stats = call(
        project_kernel,
        [wide_sheet, sheet, sheet, sheet, edge, edge, ((frames, LANES), F32)],
        (place, *token_parts, gain, weights),
        smem=(0,),
        flops=12 * square,
        moved=8 * 2**20,
    )
    kv_prev, kv_next = to_next(kv_high), to_previous(kv_low)
    span = frames + 2 * WINDOW
    attended, q_grad, kv_grad, edge_low, edge_high, gated = call(
        attention_kernel,
        [sheet, sheet, ((frames, 2 * width), F32), edge, edge, wide_sheet],
        (place, mask_wide, q_own, k_own, v_own, kv_prev, kv_next, *grad_parts, w_out),
        smem=(0,),
        scratch=[
            pltpu.VMEM((span, width), BF16),
            pltpu.VMEM((span, width), BF16),
            pltpu.VMEM((LANES, span), BF16),
            pltpu.VMEM((LANES, span), BF16),
            pltpu.VMEM((frames, width), BF16),
            pltpu.VMEM((frames // WINDOW, 3 * WINDOW, WINDOW), F32),
            pltpu.VMEM((span, width), F32),
            pltpu.VMEM((span, width), F32),
        ],
        flops=40 * square,
        moved=8 * 2**20,
    )
    from_next, from_prev = to_previous(edge_low), to_next(edge_high)
    packed = ((4, 8, 48, width), BF16)
    held = pltpu.VMEM((2, frames, width), F32)
    send, keep, *branches = call(
        first_weights_kernel,
        [packed, packed, sheet, sheet, sheet, sheet],
        (place, gated, attended, q_grad, normed, w_out),
        smem=(0,),
        scratch=[held],
        flops=12 * square,
        moved=9 * 2**20,
    )
    out_weight_grad, q_weight = scatter_sum(place, send, keep)
    branch = branches[0].astype(F32)
    for step in (1, 2, 3):
        branch = branch + shifted(branches[step], "tp", step).astype(F32)
    layer_out = (tokens.astype(F32) + frame_mask.astype(F32)[:, None] * branch).astype(BF16)

    note = ((frames + 16, width), BF16)
    send, keep, own, *norm_parts, gain_part = call(
        second_weights_kernel,
        [packed, packed, ((frames, width), F32), note, note, note, ((6, 1, width), F32)],
        (
            place, kv_grad, from_prev, from_next, q_grad, normed, weights, *token_parts, stats, gain
        ),
        smem=(0,),
        scratch=[held, pltpu.VMEM((frames, width), BF16), pltpu.VMEM((frames, width), BF16)],
        flops=20 * square,
        moved=12 * 2**20,
    )
    k_weight, v_weight = scatter_sum(place, send, keep)
    norm_received = [shifted(part, "tp", by + 1) for by, part in enumerate(norm_parts)]
    gain_own = lax.dynamic_index_in_dim(gain, place[3], 0, keepdims=False)
    (tokens_grad,) = call(
        tokens_kernel,
        [sheet],
        (gain_own, tokens, out_grad, stats, gain_part, own, *norm_received),
        moved=4 * 2**20,
    )
    gain_grad = gain_part[:4].reshape(12, LANES)
    for axis, bit in (
        ("core", 1), ("x", 1), ("x", 2), ("tp", 1), ("tp", 2), ("z", 1), ("z", 2), ("z", 4)
    ):
        gain_grad = gain_grad + swapped(gain_grad, axis, bit)
    qkv_grad = jnp.stack([q_weight, k_weight, v_weight], axis=1)
    return (layer_out, tokens_grad, gain_grad.reshape(-1), qkv_grad, out_weight_grad)


def solution(mesh):
    split = Mesh(mesh.devices.reshape(8, 4, 2, 4), ("z", "x", "core", "tp"))
    return jax.shard_map(
        per_device,
        mesh=split,
        in_specs=(P(TM, "tp"), P(), P(None, None, "tp"), P(None, "tp"), P(TM), P(TM, "tp")),
        out_specs=(P(TM, "tp"), P(TM, "tp"), P(), P(TM, None, "tp"), P(TM, "tp")),
        check_vma=False,
    )
```

```python
import jax
import jax.numpy as jnp
from jax import lax
from jax.experimental import pallas as pl
from jax.experimental.pallas import tpu as pltpu
from jax.sharding import Mesh, PartitionSpec as P

HEAD = 64
WINDOW = 128
EPSILON = 1e-05
LANES = 128
TM = ("z", "x", "core")
F32 = jnp.float32
BF16 = jnp.bfloat16


def shifted(value, axis, by):
    size = lax.axis_size(axis)
    return lax.ppermute(value, axis, [(i, (i + by) % size) for i in range(size)])


def swapped(value, axis, bit):
    size = lax.axis_size(axis)
    return lax.ppermute(value, axis, [(i, i ^ bit) for i in range(size)])


def to_next(value):
    size = lax.axis_size(TM)
    return lax.ppermute(value, TM, [(i, i + 1) for i in range(size - 1)])


def to_previous(value):
    size = lax.axis_size(TM)
    return lax.ppermute(value, TM, [(i + 1, i) for i in range(size - 1)])


def dot_nn(a, b):
    return lax.dot_general(a, b, (((1,), (0,)), ((), ())), preferred_element_type=F32)


def dot_nt(a, b):
    return lax.dot_general(a, b, (((1,), (1,)), ((), ())), preferred_element_type=F32)


def dot_tn(a, b):
    return lax.dot_general(a, b, (((0,), (0,)), ((), ())), preferred_element_type=F32)


def call(body, outs, args, smem=(), scratch=(), flops=0, moved=0, vmem=24):
    in_specs = [
        pl.BlockSpec(memory_space=pltpu.SMEM if k in smem else pltpu.VMEM) for k in range(len(args))
    ]
    return pl.pallas_call(
        body,
        out_shape=[jax.ShapeDtypeStruct(s, d) for s, d in outs],
        in_specs=in_specs,
        out_specs=[pl.BlockSpec(memory_space=pltpu.VMEM)] * len(outs),
        scratch_shapes=list(scratch),
        cost_estimate=pl.CostEstimate(flops=flops, bytes_accessed=moved, transcendentals=0),
        compiler_params=pltpu.CompilerParams(vmem_limit_bytes=vmem * 2**20),
    )(*args)


def block_of(place, step):
    return lax.rem(place[3] + step, 4)


def project_kernel(
    place, t0, t1, t2, t3, gain, weights, mask, normed, q_out, k_out, v_out, kv_low, kv_high, stats
):
    parts = (t0, t1, t2, t3)
    width = 4 * t0.shape[1]
    wide = [t[...].astype(F32) for t in parts]
    average = sum(jnp.sum(t, axis=1, keepdims=True) for t in wide) / width
    centered = [t - average for t in wide]
    variance = sum(jnp.sum(t * t, axis=1, keepdims=True) for t in centered) / width
    inverse_std = lax.rsqrt(variance + EPSILON)
    lane = lax.broadcasted_iota(jnp.int32, stats.shape, 1)
    stats[...] = jnp.where(lane == 0, average, inverse_std)
    for step in range(4):
        block = block_of(place, step)
        normed[block] = (centered[step] * inverse_std * gain[block]).astype(BF16)
    rows = t0.shape[1]
    for kind, out in enumerate((q_out, k_out, v_out)):
        total = None
        for block in range(4):
            term = dot_nn(normed[block], weights[kind, rows * block : rows * (block + 1), :])
            total = term if total is None else total + term
        out[...] = total.astype(BF16)
        if kind > 0:
            columns = slice((kind - 1) * rows, kind * rows)
            kv_low[:WINDOW, columns] = out[:WINDOW, :]
            kv_high[:WINDOW, columns] = out[out.shape[0] - WINDOW :, :]
    frames = t0.shape[0]
    for out, start in ((kv_low, 0), (kv_high, frames - WINDOW)):
        row = mask[:, start : start + WINDOW].astype(F32)
        out[WINDOW:, :LANES] = jnp.broadcast_to(row, (16, LANES)).astype(BF16)


def attention_kernel(
    place, mask, q_in, k_in, v_in, kv_prev, kv_next, g0, g1, g2, g3, w_out,
    attended, q_grad, kv_grad, kv_low, kv_high, gated,
    k_ext, v_ext, k_cross, v_cross, upstream, cap, dk_ext, dv_ext,
):
    frames, width = q_in.shape
    span = 3 * WINDOW
    blocks = frames // WINDOW
    turned = []
    for block in range(blocks + 2):
        if block == 0:
            row = kv_prev[WINDOW:, :LANES].astype(F32)[:1]
        elif block > blocks:
            row = kv_next[WINDOW:, :LANES].astype(F32)[:1]
        else:
            row = mask[:, (block - 1) * WINDOW : block * WINDOW].astype(F32)
        turned.append(jnp.transpose(jnp.broadcast_to(row, (WINDOW, WINDOW))))
    key_at = lax.broadcasted_iota(jnp.int32, (WINDOW, WINDOW), 0)
    query_at = lax.broadcasted_iota(jnp.int32, (WINDOW, WINDOW), 1)
    high, low = 3.0e38, -1e30
    for block in range(blocks):
        before = (key_at >= query_at) & (turned[block] > 0)
        inside = (key_at == query_at) | (turned[block + 1] > 0)
        after = (key_at <= query_at) & (turned[block + 2] > 0)
        for part, allowed in enumerate((before, inside, after)):
            cap[block, part * WINDOW : (part + 1) * WINDOW, :] = jnp.where(allowed, high, low)

    total = None
    for step, ref in enumerate((g0, g1, g2, g3)):
        block = block_of(place, step)
        for part in range(blocks):
            rows = slice(part * WINDOW, (part + 1) * WINDOW)
            keep = turned[part + 1]
            keep = jnp.concatenate([keep] * (width // WINDOW), axis=1)
            gated[block, rows, :] = (ref[rows, :].astype(F32) * keep).astype(BF16)
    for block in range(4):
        term = dot_nn(gated[block], w_out[width * block : width * (block + 1), :])
        total = term if total is None else total + term
    upstream[...] = total.astype(BF16)

    for ext, own, at in ((k_ext, k_in, 0), (v_ext, v_in, width)):
        ext[:WINDOW, :] = kv_prev[:WINDOW, at : at + width]
        ext[WINDOW : WINDOW + frames, :] = own[...]
        ext[WINDOW + frames :, :] = kv_next[:WINDOW, at : at + width]
    dk_ext[...] = jnp.zeros_like(dk_ext)
    dv_ext[...] = jnp.zeros_like(dv_ext)
    scaling = HEAD ** (-0.5)
    first = lax.broadcasted_iota(jnp.int32, (WINDOW, LANES), 1) < HEAD
    for pair in range(width // LANES):
        lanes = slice(pair * LANES, (pair + 1) * LANES)
        k_cross[...] = jnp.transpose(k_ext[:, lanes].astype(F32) * scaling).astype(BF16)
        v_cross[...] = jnp.transpose(v_ext[:, lanes].astype(F32)).astype(BF16)
        for block in range(blocks):
            rows = slice(block * WINDOW, (block + 1) * WINDOW)
            keys = slice(block * WINDOW, block * WINDOW + span)
            query = q_in[rows, lanes] * jnp.asarray(scaling, BF16)
            zero = jnp.zeros_like(query)
            query = jnp.concatenate(
                [jnp.where(first, query, zero), jnp.where(first, zero, query)], axis=0
            )
            grad = upstream[rows, lanes]
            grad = jnp.concatenate(
                [jnp.where(first, grad, zero), jnp.where(first, zero, grad)], axis=0
            )
            bound = cap[block]
            bound = jnp.concatenate([bound, bound], axis=1)
            scores = jnp.minimum(dot_nt(k_ext[keys, lanes], query), bound)
            largest = jnp.max(scores, axis=0, keepdims=True)
            exponent = jnp.exp(scores - largest)
            probability = exponent * (1.0 / jnp.sum(exponent, axis=0, keepdims=True))
            probability_low = probability.astype(BF16)
            probability_grad = dot_nt(v_ext[keys, lanes], grad)
            row_dots = jnp.sum(probability * probability_grad, axis=0, keepdims=True)
            score_grad = (probability * (probability_grad - row_dots)).astype(BF16)
            dv_ext[keys, lanes] += dot_nn(probability_low, grad)
            dk_ext[keys, lanes] += dot_nn(score_grad, query)
            for cross, factor, out in (
                (v_cross, probability_low, attended),
                (k_cross, score_grad, q_grad),
            ):
                both = dot_nn(cross[:, keys], factor)
                both = jnp.concatenate([both[:HEAD, :WINDOW], both[HEAD:, WINDOW:]], axis=0)
                out[rows, lanes] = jnp.transpose(both).astype(BF16)
    for ext, at in ((dk_ext, 0), (dv_ext, width)):
        columns = slice(at, at + width)
        kv_low[:, columns] = ext[:WINDOW, :].astype(BF16)
        kv_grad[:, columns] = ext[WINDOW : WINDOW + frames, :]
        kv_high[:, columns] = ext[WINDOW + frames :, :].astype(BF16)


def split_rows(place, block, held, send, keep):
    core = place[2]
    for group in range(8):
        at = group % 4 * 8 + 2 * block + group // 4
        for out, whose in ((send, 1 - core), (keep, core)):
            start = pl.multiple_of(48 * group + 24 * whose, 8)
            both = jnp.concatenate([held[0, pl.ds(start, 24), :], held[1, pl.ds(start, 24), :]], 0)
            out[at] = both.astype(BF16)


def folded(value):
    return value[:, :LANES] + value[:, LANES : 2 * LANES] + value[:, 2 * LANES :]


def in_two(value):
    head = value.astype(BF16).astype(F32)
    return jnp.concatenate([head, value - head], axis=0).astype(BF16)


def from_two(value):
    wide = value.astype(F32)
    return wide[:8] + wide[8:16]


def first_weights_kernel(
    place, gated, attended, q_grad, normed, weights, send, keep, gain_sums, held
):
    width = attended.shape[1]
    for block in range(4):
        rows = slice(width * block, width * (block + 1))
        held[0] = dot_tn(gated[block], attended[...])
        held[1] = dot_tn(normed[block], q_grad[...])
        gain_sums[block] = folded(held[1] * weights[0, rows, :].astype(F32))
        split_rows(place, block, held, send, keep)


def second_weights_kernel(
    place, kv_grad, from_prev, from_next, normed, weights, gain_sums, gain,
    send, keep, k_grad, v_grad, gain_part, held,
):
    frames, width = k_grad.shape
    for out, at in ((k_grad, 0), (v_grad, width)):
        columns = slice(at, at + width)
        out[:WINDOW, :] = (
            kv_grad[:WINDOW, columns] + from_prev[:, columns].astype(F32)
        ).astype(BF16)
        out[WINDOW : frames - WINDOW, :] = kv_grad[WINDOW : frames - WINDOW, columns].astype(BF16)
        out[frames - WINDOW :, :] = (
            kv_grad[frames - WINDOW :, columns] + from_next[:, columns].astype(F32)
        ).astype(BF16)
    gain_part[...] = jnp.zeros_like(gain_part)
    for block in range(4):
        rows = slice(width * block, width * (block + 1))
        held[0] = dot_tn(normed[block], k_grad[...])
        held[1] = dot_tn(normed[block], v_grad[...])
        sums = gain_sums[block] + folded(
            held[0] * weights[1, rows, :].astype(F32) + held[1] * weights[2, rows, :].astype(F32)
        )
        for part in range(width // LANES):
            lanes = slice(part * LANES, (part + 1) * LANES)
            turned = jnp.transpose(sums[lanes, :])
            row = jnp.sum(turned, axis=0, keepdims=True)
            gain_part[block : block + 1, lanes] = row / gain[block][:, lanes]
        split_rows(place, block, held, send, keep)
    send[32, :16, :] = in_two(gain_part[...])


def norm_kernel(after, attended, w_out, q_grad, k_grad, v_grad, weights, normed, gain, parts):
    del after
    frames, width = q_grad.shape
    first_sum = second_sum = None
    for block in range(4):
        rows = slice(width * block, width * (block + 1))
        total = None
        for kind, part in enumerate((q_grad, k_grad, v_grad)):
            term = dot_nt(part[...], weights[kind, rows, :])
            total = term if total is None else total + term
        parts[block, :frames, :] = total.astype(BF16)
        branch = dot_nt(attended[...], w_out[rows, :])
        parts[block, frames + 16 :, :] = branch.astype(BF16)
        first = jnp.sum(total * gain[block], axis=1, keepdims=True)
        second = jnp.sum(total * normed[block].astype(F32), axis=1, keepdims=True)
        first_sum = first if first_sum is None else first_sum + first
        second_sum = second if second_sum is None else second_sum + second
    lane = lax.broadcasted_iota(jnp.int32, (frames, LANES), 1)
    sums = jnp.transpose(jnp.where(lane == 0, first_sum, jnp.where(lane == 1, second_sum, 0.0)))
    tail = in_two(sums[:8, :])
    for block in range(4):
        parts[block, frames : frames + 16, :] = tail


def tokens_kernel(place, gain, tokens, out_grad, stats, parts, out):
    frames = tokens.shape[0]
    width = 4 * tokens.shape[1]
    average, inverse_std = stats[:, 0:1], stats[:, 1:2]
    total, rows = None, None
    for block in range(4):
        part = parts[block, :frames, :].astype(F32)
        tail = from_two(parts[block, frames : frames + 16, :])
        total = part if total is None else total + part
        rows = tail if rows is None else rows + tail
    rows = jnp.concatenate([rows, jnp.zeros((LANES - 8, frames), F32)], axis=0) / width
    turned = jnp.transpose(rows)
    first_mean, second_mean = turned[:, 0:1], turned[:, 1:2]
    whitened = (tokens[...].astype(F32) - average) * inverse_std
    unit = total * gain[place[3]]
    moved = (unit - first_mean - whitened * second_mean) * inverse_std
    out[...] = (out_grad[...].astype(F32) + moved).astype(BF16)


def layer_kernel(tokens, mask, parts, out):
    total = None
    for block in range(4):
        term = parts[block, tokens.shape[0] + 16 :, :].astype(F32)
        total = term if total is None else total + term
    for part in range(tokens.shape[0] // WINDOW):
        rows = slice(part * WINDOW, (part + 1) * WINDOW)
        row = mask[:, rows].astype(F32)
        keep = jnp.transpose(jnp.broadcast_to(row, (WINDOW, WINDOW)))
        keep = jnp.concatenate([keep] * (tokens.shape[1] // WINDOW), axis=1)
        out[rows, :] = (tokens[rows, :].astype(F32) + keep * total[rows, :]).astype(BF16)


def core_sum(place, keep, received, outs):
    for step, out in enumerate(outs):
        for z in range(8):
            which = lax.rem(place[1] + step, 4) * 8 + z
            out[z] = (keep[which].astype(F32) + received[which].astype(F32)).astype(out.dtype)


def first_core_kernel(place, keep, received, own, p1, p2, p3):
    core_sum(place, keep, received, (own, p1, p2, p3))


def second_core_kernel(place, keep, received, gain_part, own, p1, p2, p3, gain_sum):
    core_sum(place, keep, received, (own, p1, p2, p3))
    gain_sum[...] = from_two(in_two(gain_part[...])) + from_two(received[32, :16, :])
    for out in (p1, p2, p3):
        out[8, :16, :] = in_two(gain_sum[...])


def x_sum_kernel(
    place, own1, a1, a2, a3, own2, b1, b2, b3, gain_part, send, keep, gain_sum
):
    parity = lax.rem(place[0], 2)
    for out, whose in ((send, 1 - parity), (keep, parity)):
        for far in range(4):
            for at, (own, r1, r2, r3) in enumerate(((own1, a1, a2, a3), (own2, b1, b2, b3))):
                which = 2 * far + whose
                total = own[which] + r2[which].astype(F32)
                total = total + (r1[which].astype(F32) + r3[which].astype(F32))
                start = 96 * far + 48 * at
                out[start : start + 48, :] = total.astype(out.dtype)
    near = from_two(in_two(gain_part[...])) + from_two(b2[8, :16, :])
    gain_sum[...] = near + (from_two(b1[8, :16, :]) + from_two(b3[8, :16, :]))
    send[384:, :] = in_two(gain_sum[...])


def near_sum_kernel(place, keep, received, gain_part, own, p1, p2, p3, gain_sum):
    far = lax.div(place[0], 2)
    gain_sum[...] = from_two(in_two(gain_part[...])) + from_two(received[384:, :])
    for step, out in enumerate((own, p1, p2, p3)):
        rows = pl.ds(pl.multiple_of(96 * lax.rem(far + step, 4), 32), 96)
        total = keep[rows, :] + received[rows, :].astype(F32)
        out[:96, :] = total.astype(out.dtype)
        if step:
            out[96:, :] = in_two(gain_sum[...])


def far_sum_kernel(own, r1, r2, r3, gain_part, out_weight, qkv_weight, gain_sum):
    total = own[...] + r2[:96, :].astype(F32)
    total = total + (r1[:96, :].astype(F32) + r3[:96, :].astype(F32))
    out_weight[...] = total[:24]
    for kind in range(3):
        qkv_weight[kind] = total[24 * (kind + 1) : 24 * (kind + 2)]
    near = from_two(in_two(gain_part[...])) + from_two(r2[96:, :])
    gain_sum[...] = (near + (from_two(r1[96:, :]) + from_two(r3[96:, :])))[:4]


def per_device(tokens, ln_gain, w_qkv, w_out, frame_mask, out_grad):
    frames, width = tokens.shape
    place = jnp.stack([lax.axis_index(a) for a in ("z", "x", "core", "tp")]).astype(jnp.int32)
    token_parts = [tokens] + [shifted(tokens, "tp", -step) for step in (1, 2, 3)]
    late, token_parts[1:] = lax.optimization_barrier((out_grad, token_parts[1:]))
    grad_parts = [out_grad] + [shifted(late, "tp", -step) for step in (1, 2, 3)]
    mask_row = frame_mask[None, :]
    gain = ln_gain.reshape(4, 1, width)
    weights = jnp.transpose(w_qkv, (1, 0, 2))

    sheet, wide_sheet = ((frames, width), BF16), ((4, frames, width), BF16)
    edge, halo = ((WINDOW, 2 * width), BF16), ((WINDOW + 16, 2 * width), BF16)
    square = frames * width * width * 2
    normed, q_own, k_own, v_own, kv_low, kv_high, stats = call(
        project_kernel,
        [wide_sheet, sheet, sheet, sheet, halo, halo, ((frames, LANES), F32)],
        (place, *token_parts, gain, weights, mask_row),
        smem=(0,),
        flops=12 * square,
        moved=8 * 2**20,
    )
    kv_prev, kv_next = to_next(kv_high), to_previous(kv_low)
    span = frames + 2 * WINDOW
    attended, q_grad, kv_grad, edge_low, edge_high, gated = call(
        attention_kernel,
        [sheet, sheet, ((frames, 2 * width), F32), edge, edge, wide_sheet],
        (place, mask_row, q_own, k_own, v_own, kv_prev, kv_next, *grad_parts, w_out),
        smem=(0,),
        scratch=[
            pltpu.VMEM((span, width), BF16),
            pltpu.VMEM((span, width), BF16),
            pltpu.VMEM((LANES, span), BF16),
            pltpu.VMEM((LANES, span), BF16),
            pltpu.VMEM((frames, width), BF16),
            pltpu.VMEM((frames // WINDOW, 3 * WINDOW, WINDOW), F32),
            pltpu.VMEM((span, width), F32),
            pltpu.VMEM((span, width), F32),
        ],
        flops=40 * square,
        moved=8 * 2**20,
    )
    from_next, from_prev = to_previous(edge_low), to_next(edge_high)
    held = pltpu.VMEM((2, frames, width), F32)

    def pieces(count, dtype=BF16):
        return ((count, 48, width), dtype)

    small = ((8, width), F32)
    send, keep, gain_sums = call(
        first_weights_kernel,
        [pieces(32), pieces(32), ((4, frames, LANES), F32)],
        (place, gated, attended, q_grad, normed, weights),
        smem=(0,),
        scratch=[held],
        flops=12 * square,
        moved=9 * 2**20,
    )
    received = swapped(send, "core", 1)
    send2, keep2, k_grad, v_grad, gain_part = call(
        second_weights_kernel,
        [pieces(33), pieces(32), sheet, sheet, small],
        (place, kv_grad, from_prev, from_next, normed, weights, gain_sums, gain),
        smem=(0,),
        scratch=[held],
        flops=12 * square,
        moved=9 * 2**20,
    )
    received2 = swapped(send2, "core", 1)
    own1, *parts = call(
        first_core_kernel,
        [pieces(8, F32)] + [pieces(8)] * 3,
        (place, keep, received),
        smem=(0,),
        moved=6 * 2**20,
        vmem=16,
    )
    received1 = [shifted(part, "x", by + 1) for by, part in enumerate(parts)]
    own2, *parts, gain_part = call(
        second_core_kernel,
        [pieces(8, F32)] + [pieces(9)] * 3 + [small],
        (place, keep2, received2, gain_part),
        smem=(0,),
        moved=6 * 2**20,
        vmem=16,
    )
    received2 = [shifted(part, "x", by + 1) for by, part in enumerate(parts)]
    (exchanged,) = call(
        norm_kernel,
        [((4, 2 * frames + 16, width), BF16)],
        (gain_part, attended, w_out, q_grad, k_grad, v_grad, weights, normed, gain),
        flops=16 * square,
        moved=9 * 2**20,
    )
    exchanged = lax.all_to_all(exchanged, "tp", 0, 0, tiled=True)
    send, keep, gain_part = call(
        x_sum_kernel,
        [((400, width), BF16), ((384, width), F32), small],
        (place, own1, *received1, own2, *received2, gain_part),
        smem=(0,),
        moved=6 * 2**20,
        vmem=16,
    )
    received = swapped(send, "z", 1)
    (layer_out,) = call(
        layer_kernel, [sheet], (tokens, mask_row, exchanged), moved=2 * 2**20, vmem=16
    )
    (tokens_grad,) = call(
        tokens_kernel,
        [sheet],
        (place, gain, tokens, out_grad, stats, exchanged),
        smem=(0,),
        moved=4 * 2**20,
        vmem=16,
    )
    own, *parts, gain_part = call(
        near_sum_kernel,
        [((96, width), F32)] + [((112, width), BF16)] * 3 + [small],
        (place, keep, received, gain_part),
        smem=(0,),
        moved=2**20,
        vmem=16,
    )
    received = [shifted(part, "z", 2 * (by + 1)) for by, part in enumerate(parts)]
    out_weight_grad, qkv_grad, gain_part = call(
        far_sum_kernel,
        [((24, width), F32), ((3, 24, width), F32), ((4, width), F32)],
        (own, *received, gain_part),
        moved=2**20,
        vmem=16,
    )
    around = [shifted(gain_part, "tp", by) for by in (1, 2, 3)]
    gain_grad = (gain_part + around[1]) + (around[0] + around[2])
    return (
        layer_out,
        tokens_grad,
        gain_grad.reshape(-1),
        jnp.transpose(qkv_grad, (1, 0, 2)),
        out_weight_grad,
    )


def solution(mesh):
    split = Mesh(mesh.devices.reshape(8, 4, 2, 4), ("z", "x", "core", "tp"))
    return jax.shard_map(
        per_device,
        mesh=split,
        in_specs=(P(TM, "tp"), P(), P(None, None, "tp"), P(None, "tp"), P(TM), P(TM, "tp")),
        out_specs=(P(TM, "tp"), P(TM, "tp"), P(), P(TM, None, "tp"), P(TM, "tp")),
        check_vma=False,
    )
```

```python
import jax
import jax.numpy as jnp
from jax import lax
from jax.experimental import pallas as pl
from jax.experimental.pallas import tpu as pltpu
from jax.sharding import Mesh, PartitionSpec as P

HEAD = 64
WINDOW = 128
EPSILON = 1e-05
LANES = 128
TM = ("z", "x", "core")
F32 = jnp.float32
BF16 = jnp.bfloat16


def shifted(value, axis, by):
    size = lax.axis_size(axis)
    return lax.ppermute(value, axis, [(i, (i + by) % size) for i in range(size)])


def swapped(value, axis, bit):
    size = lax.axis_size(axis)
    return lax.ppermute(value, axis, [(i, i ^ bit) for i in range(size)])


def to_next(value):
    size = lax.axis_size(TM)
    return lax.ppermute(value, TM, [(i, i + 1) for i in range(size - 1)])


def to_previous(value):
    size = lax.axis_size(TM)
    return lax.ppermute(value, TM, [(i + 1, i) for i in range(size - 1)])


def dot_nn(a, b):
    return lax.dot_general(a, b, (((1,), (0,)), ((), ())), preferred_element_type=F32)


def dot_nt(a, b):
    return lax.dot_general(a, b, (((1,), (1,)), ((), ())), preferred_element_type=F32)


def dot_tn(a, b):
    return lax.dot_general(a, b, (((0,), (0,)), ((), ())), preferred_element_type=F32)


def call(body, outs, args, smem=(), far=(), scratch=(), cost=0, vmem=24):
    in_specs = [
        pl.BlockSpec(
            memory_space=pltpu.SMEM if k in smem else pltpu.HBM if k in far else pltpu.VMEM
        )
        for k in range(len(args))
    ]
    return pl.pallas_call(
        body,
        out_shape=[jax.ShapeDtypeStruct(s, d) for s, d in outs],
        in_specs=in_specs,
        out_specs=[pl.BlockSpec(memory_space=pltpu.VMEM)] * len(outs),
        scratch_shapes=list(scratch),
        cost_estimate=pl.CostEstimate(flops=cost, bytes_accessed=0, transcendentals=0),
        compiler_params=pltpu.CompilerParams(vmem_limit_bytes=vmem * 2**20),
    )(*args)


def block_of(place, step):
    return lax.rem(place[3] + step, 4)


def preload_kernel(weights, tokens, weights_here, tokens_here, arrived):
    first = pltpu.make_async_copy(weights, weights_here, arrived.at[0])
    second = pltpu.make_async_copy(tokens, tokens_here, arrived.at[1])
    first.start()
    second.start()
    first.wait()
    second.wait()


def project_kernel(
    place, t0, t1, t2, t3, gain, weights, mask, normed, q_out, k_out, v_out, kv_low, kv_high, stats
):
    parts = (t0, t1, t2, t3)
    width = 4 * t0.shape[1]
    wide = [t[...].astype(F32) for t in parts]
    average = sum(jnp.sum(t, axis=1, keepdims=True) for t in wide) / width
    centered = [t - average for t in wide]
    variance = sum(jnp.sum(t * t, axis=1, keepdims=True) for t in centered) / width
    inverse_std = lax.rsqrt(variance + EPSILON)
    lane = lax.broadcasted_iota(jnp.int32, stats.shape, 1)
    stats[...] = jnp.where(lane == 0, average, inverse_std)
    for step in range(4):
        block = block_of(place, step)
        normed[block] = (centered[step] * inverse_std * gain[block]).astype(BF16)
    rows = t0.shape[1]
    for kind, out in enumerate((q_out, k_out, v_out)):
        total = None
        for block in range(4):
            term = dot_nn(normed[block], weights[kind, rows * block : rows * (block + 1), :])
            total = term if total is None else total + term
        out[...] = total.astype(BF16)
        if kind > 0:
            columns = slice((kind - 1) * rows, kind * rows)
            kv_low[:WINDOW, columns] = out[:WINDOW, :]
            kv_high[:WINDOW, columns] = out[out.shape[0] - WINDOW :, :]
    frames = t0.shape[0]
    for out, start in ((kv_low, 0), (kv_high, frames - WINDOW)):
        row = mask[:, start : start + WINDOW].astype(F32)
        out[WINDOW:, :LANES] = jnp.broadcast_to(row, (16, LANES)).astype(BF16)


def attention_kernel(
    place, mask, q_in, k_in, v_in, kv_prev, kv_next, g0, g1, g2, g3, w_out,
    attended, q_grad, kv_grad, kv_low, kv_high, gated,
    k_ext, v_ext, k_cross, v_cross, upstream, cap, dk_ext, dv_ext,
):
    frames, width = q_in.shape
    span = 3 * WINDOW
    blocks = frames // WINDOW
    turned = []
    for block in range(blocks + 2):
        if block == 0:
            row = kv_prev[WINDOW:, :LANES].astype(F32)[:1]
        elif block > blocks:
            row = kv_next[WINDOW:, :LANES].astype(F32)[:1]
        else:
            row = mask[:, (block - 1) * WINDOW : block * WINDOW].astype(F32)
        turned.append(jnp.transpose(jnp.broadcast_to(row, (WINDOW, WINDOW))))
    key_at = lax.broadcasted_iota(jnp.int32, (WINDOW, WINDOW), 0)
    query_at = lax.broadcasted_iota(jnp.int32, (WINDOW, WINDOW), 1)
    high, low = 3.0e38, -1e30
    for block in range(blocks):
        before = (key_at >= query_at) & (turned[block] > 0)
        inside = (key_at == query_at) | (turned[block + 1] > 0)
        after = (key_at <= query_at) & (turned[block + 2] > 0)
        for part, allowed in enumerate((before, inside, after)):
            cap[block, part * WINDOW : (part + 1) * WINDOW, :] = jnp.where(allowed, high, low)

    total = None
    for step, ref in enumerate((g0, g1, g2, g3)):
        block = block_of(place, step)
        for part in range(blocks):
            rows = slice(part * WINDOW, (part + 1) * WINDOW)
            keep = turned[part + 1]
            keep = jnp.concatenate([keep] * (width // WINDOW), axis=1)
            gated[block, rows, :] = (ref[rows, :].astype(F32) * keep).astype(BF16)
    for block in range(4):
        term = dot_nn(gated[block], w_out[width * block : width * (block + 1), :])
        total = term if total is None else total + term
    upstream[...] = total.astype(BF16)

    for ext, own, at in ((k_ext, k_in, 0), (v_ext, v_in, width)):
        ext[:WINDOW, :] = kv_prev[:WINDOW, at : at + width]
        ext[WINDOW : WINDOW + frames, :] = own[...]
        ext[WINDOW + frames :, :] = kv_next[:WINDOW, at : at + width]
    dk_ext[...] = jnp.zeros_like(dk_ext)
    dv_ext[...] = jnp.zeros_like(dv_ext)
    scaling = HEAD ** (-0.5)
    first = lax.broadcasted_iota(jnp.int32, (WINDOW, LANES), 1) < HEAD
    for pair in range(width // LANES):
        lanes = slice(pair * LANES, (pair + 1) * LANES)
        k_cross[...] = jnp.transpose(k_ext[:, lanes].astype(F32) * scaling).astype(BF16)
        v_cross[...] = jnp.transpose(v_ext[:, lanes].astype(F32)).astype(BF16)
        for block in range(blocks):
            rows = slice(block * WINDOW, (block + 1) * WINDOW)
            keys = slice(block * WINDOW, block * WINDOW + span)
            query = q_in[rows, lanes] * jnp.asarray(scaling, BF16)
            zero = jnp.zeros_like(query)
            query = jnp.concatenate(
                [jnp.where(first, query, zero), jnp.where(first, zero, query)], axis=0
            )
            grad = upstream[rows, lanes]
            grad = jnp.concatenate(
                [jnp.where(first, grad, zero), jnp.where(first, zero, grad)], axis=0
            )
            bound = cap[block]
            bound = jnp.concatenate([bound, bound], axis=1)
            scores = jnp.minimum(dot_nt(k_ext[keys, lanes], query), bound)
            largest = jnp.max(scores, axis=0, keepdims=True)
            exponent = jnp.exp(scores - largest)
            probability = exponent * (1.0 / jnp.sum(exponent, axis=0, keepdims=True))
            probability_low = probability.astype(BF16)
            probability_grad = dot_nt(v_ext[keys, lanes], grad)
            row_dots = jnp.sum(probability * probability_grad, axis=0, keepdims=True)
            score_grad = (probability * (probability_grad - row_dots)).astype(BF16)
            dv_ext[keys, lanes] += dot_nn(probability_low, grad)
            dk_ext[keys, lanes] += dot_nn(score_grad, query)
            for cross, factor, out in (
                (v_cross, probability_low, attended),
                (k_cross, score_grad, q_grad),
            ):
                both = dot_nn(cross[:, keys], factor)
                both = jnp.concatenate([both[:HEAD, :WINDOW], both[HEAD:, WINDOW:]], axis=0)
                out[rows, lanes] = jnp.transpose(both).astype(BF16)
    for ext, at in ((dk_ext, 0), (dv_ext, width)):
        columns = slice(at, at + width)
        kv_low[:, columns] = ext[:WINDOW, :].astype(BF16)
        kv_grad[:, columns] = ext[WINDOW : WINDOW + frames, :]
        kv_high[:, columns] = ext[WINDOW + frames :, :].astype(BF16)


def split_rows(place, block, held, send, keep):
    core = place[2]
    for group in range(8):
        at = group % 4 * 8 + 2 * block + group // 4
        for out, whose in ((send, 1 - core), (keep, core)):
            start = pl.multiple_of(48 * group + 24 * whose, 8)
            both = jnp.concatenate([held[0, pl.ds(start, 24), :], held[1, pl.ds(start, 24), :]], 0)
            out[at] = both.astype(BF16)


def folded(value):
    return value[:, :LANES] + value[:, LANES : 2 * LANES] + value[:, 2 * LANES :]


def in_two(value):
    head = value.astype(BF16).astype(F32)
    return jnp.concatenate([head, value - head], axis=0).astype(BF16)


def from_two(value):
    wide = value.astype(F32)
    return wide[:8] + wide[8:16]


def first_weights_kernel(
    place, gated, attended, q_grad, normed, weights, send, keep, gain_sums, held
):
    width = attended.shape[1]
    for block in range(4):
        rows = slice(width * block, width * (block + 1))
        held[0] = dot_tn(gated[block], attended[...])
        held[1] = dot_tn(normed[block], q_grad[...])
        gain_sums[block] = folded(held[1] * weights[0, rows, :].astype(F32))
        split_rows(place, block, held, send, keep)


def branch_kernel(attended, w_out, branches):
    width = attended.shape[1]
    for block in range(4):
        rows = w_out[width * block : width * (block + 1), :]
        branches[block] = dot_nt(attended[...], rows).astype(BF16)


def second_weights_kernel(
    place, kv_grad, from_prev, from_next, normed, weights, gain_sums, gain,
    send, keep, k_grad, v_grad, gain_part, held,
):
    frames, width = k_grad.shape
    for out, at in ((k_grad, 0), (v_grad, width)):
        columns = slice(at, at + width)
        out[:WINDOW, :] = (
            kv_grad[:WINDOW, columns] + from_prev[:, columns].astype(F32)
        ).astype(BF16)
        out[WINDOW : frames - WINDOW, :] = kv_grad[WINDOW : frames - WINDOW, columns].astype(BF16)
        out[frames - WINDOW :, :] = (
            kv_grad[frames - WINDOW :, columns] + from_next[:, columns].astype(F32)
        ).astype(BF16)
    gain_part[...] = jnp.zeros_like(gain_part)
    for block in range(4):
        rows = slice(width * block, width * (block + 1))
        held[0] = dot_tn(normed[block], k_grad[...])
        held[1] = dot_tn(normed[block], v_grad[...])
        sums = gain_sums[block] + folded(
            held[0] * weights[1, rows, :].astype(F32) + held[1] * weights[2, rows, :].astype(F32)
        )
        for part in range(width // LANES):
            lanes = slice(part * LANES, (part + 1) * LANES)
            turned = jnp.transpose(sums[lanes, :])
            row = jnp.sum(turned, axis=0, keepdims=True)
            gain_part[block : block + 1, lanes] = row / gain[block][:, lanes]
        split_rows(place, block, held, send, keep)
    send[32, :16, :] = in_two(gain_part[...])


def norm_kernel(
    place, branches, q_grad, k_grad, v_grad, weights, normed, gain, n0, n1, n2, n3
):
    frames, width = q_grad.shape
    first_sum = second_sum = None
    for step, out in enumerate((n0, n1, n2, n3)):
        block = block_of(place, step)
        rows = pl.ds(pl.multiple_of(width * block, width), width)
        total = None
        for kind, part in enumerate((q_grad, k_grad, v_grad)):
            term = dot_nt(part[...], weights[kind, rows, :])
            total = term if total is None else total + term
        out[:frames, :] = total.astype(BF16)
        out[frames + 16 :, :] = branches[block]
        first = jnp.sum(total * gain[block], axis=1, keepdims=True)
        second = jnp.sum(total * normed[block].astype(F32), axis=1, keepdims=True)
        first_sum = first if first_sum is None else first_sum + first
        second_sum = second if second_sum is None else second_sum + second
    lane = lax.broadcasted_iota(jnp.int32, (frames, LANES), 1)
    sums = jnp.transpose(jnp.where(lane == 0, first_sum, jnp.where(lane == 1, second_sum, 0.0)))
    tail = in_two(sums[:8, :])
    for out in (n0, n1, n2, n3):
        out[frames : frames + 16, :] = tail


def tokens_kernel(place, gain, tokens, out_grad, stats, n0, n1, n2, n3, out):
    frames = tokens.shape[0]
    width = 4 * tokens.shape[1]
    average, inverse_std = stats[:, 0:1], stats[:, 1:2]
    total, rows = None, None
    for ref in (n0, n1, n2, n3):
        part = ref[:frames, :].astype(F32)
        tail = from_two(ref[frames : frames + 16, :])
        total = part if total is None else total + part
        rows = tail if rows is None else rows + tail
    rows = jnp.concatenate([rows, jnp.zeros((LANES - 8, frames), F32)], axis=0) / width
    turned = jnp.transpose(rows)
    first_mean, second_mean = turned[:, 0:1], turned[:, 1:2]
    whitened = (tokens[...].astype(F32) - average) * inverse_std
    unit = total * gain[place[3]]
    moved = (unit - first_mean - whitened * second_mean) * inverse_std
    out[...] = (out_grad[...].astype(F32) + moved).astype(BF16)


def layer_kernel(tokens, mask, n0, n1, n2, n3, out):
    total = None
    for ref in (n0, n1, n2, n3):
        term = ref[tokens.shape[0] + 16 :, :].astype(F32)
        total = term if total is None else total + term
    for part in range(tokens.shape[0] // WINDOW):
        rows = slice(part * WINDOW, (part + 1) * WINDOW)
        row = mask[:, rows].astype(F32)
        keep = jnp.transpose(jnp.broadcast_to(row, (WINDOW, WINDOW)))
        keep = jnp.concatenate([keep] * (tokens.shape[1] // WINDOW), axis=1)
        out[rows, :] = (tokens[rows, :].astype(F32) + keep * total[rows, :]).astype(BF16)


def core_sum(place, keep, received, outs):
    for step, out in enumerate(outs):
        for z in range(8):
            which = lax.rem(place[1] + step, 4) * 8 + z
            out[z] = (keep[which].astype(F32) + received[which].astype(F32)).astype(out.dtype)


def first_core_kernel(place, keep, received, send, own):
    parity = lax.rem(place[0], 2)
    for out, whose in ((send, 1 - parity), (own, parity)):
        for x in range(4):
            for far in range(4):
                which = 8 * x + 2 * far + whose
                total = keep[which].astype(F32) + received[which].astype(F32)
                out[4 * x + far] = total.astype(out.dtype)


def second_core_kernel(place, keep, received, gain_part, own, p1, p2, p3, gain_sum):
    core_sum(place, keep, received, (own, p1, p2, p3))
    gain_sum[...] = from_two(in_two(gain_part[...])) + from_two(received[32, :16, :])
    for out in (p1, p2, p3):
        out[8, :16, :] = in_two(gain_sum[...])


def first_near_kernel(place, keep, received, own, p1, p2, p3):
    for step, out in enumerate((own, p1, p2, p3)):
        for far in range(4):
            which = lax.rem(place[1] + step, 4) * 4 + far
            out[far] = (keep[which] + received[which].astype(F32)).astype(out.dtype)


def second_x_kernel(place, own, r1, r2, r3, gain_part, send, keep, gain_sum):
    parity = lax.rem(place[0], 2)
    for out, whose in ((send, 1 - parity), (keep, parity)):
        for far in range(4):
            which = 2 * far + whose
            total = own[which] + r2[which].astype(F32)
            total = total + (r1[which].astype(F32) + r3[which].astype(F32))
            out[48 * far : 48 * far + 48, :] = total.astype(out.dtype)
    near = from_two(in_two(gain_part[...])) + from_two(r2[8, :16, :])
    gain_sum[...] = near + (from_two(r1[8, :16, :]) + from_two(r3[8, :16, :]))
    send[192:, :] = in_two(gain_sum[...])


def near_sum_kernel(
    place, own1, r1, r2, r3, keep, received, gain_part, own, p1, p2, p3, gain_sum
):
    gain_sum[...] = from_two(in_two(gain_part[...])) + from_two(received[192:, :])
    for step, out in enumerate((own, p1, p2, p3)):
        far = lax.rem(lax.div(place[0], 2) + step, 4)
        first = own1[far] + r2[far].astype(F32)
        first = first + (r1[far].astype(F32) + r3[far].astype(F32))
        rows = pl.ds(pl.multiple_of(48 * far, 16), 48)
        second = keep[rows, :] + received[rows, :].astype(F32)
        out[:48, :] = first.astype(out.dtype)
        out[48:96, :] = second.astype(out.dtype)
        if step:
            out[96:, :] = in_two(gain_sum[...])


def far_sum_kernel(own, r1, r2, r3, gain_part, out_weight, qkv_weight, gain_sum):
    total = own[...] + r2[:96, :].astype(F32)
    total = total + (r1[:96, :].astype(F32) + r3[:96, :].astype(F32))
    out_weight[...] = total[:24]
    for kind in range(3):
        qkv_weight[kind] = total[24 * (kind + 1) : 24 * (kind + 2)]
    near = from_two(in_two(gain_part[...])) + from_two(r2[96:, :])
    gain_sum[...] = (near + (from_two(r1[96:, :]) + from_two(r3[96:, :])))[:4]


def per_device(tokens, ln_gain, w_qkv, w_out, frame_mask, out_grad):
    frames, width = tokens.shape
    place = jnp.stack([lax.axis_index(a) for a in ("z", "x", "core", "tp")]).astype(jnp.int32)
    token_parts = [tokens] + [shifted(tokens, "tp", -step) for step in (1, 2, 3)]
    late, token_parts[3] = lax.optimization_barrier((out_grad, token_parts[3]))
    grad_parts = [out_grad] + [shifted(late, "tp", -step) for step in (1, 2, 3)]
    mask_row = frame_mask[None, :]
    gain = ln_gain.reshape(4, 1, width)
    weights = jnp.transpose(w_qkv, (1, 0, 2))
    weights_here, token_parts[0] = call(
        preload_kernel,
        [(weights.shape, BF16), ((frames, width), BF16)],
        (weights, tokens),
        far=(0, 1),
        scratch=[pltpu.SemaphoreType.DMA((2,))],
        cost=2**30,
        vmem=8,
    )

    sheet, wide_sheet = ((frames, width), BF16), ((4, frames, width), BF16)
    edge, halo = ((WINDOW, 2 * width), BF16), ((WINDOW + 16, 2 * width), BF16)
    square = frames * width * width * 2
    normed, q_own, k_own, v_own, kv_low, kv_high, stats = call(
        project_kernel,
        [wide_sheet, sheet, sheet, sheet, halo, halo, ((frames, LANES), F32)],
        (place, *token_parts, gain, weights_here, mask_row),
        smem=(0,),
        cost=12 * square,
    )
    kv_prev, kv_next = to_next(kv_high), to_previous(kv_low)
    span = frames + 2 * WINDOW
    attended, q_grad, kv_grad, edge_low, edge_high, gated = call(
        attention_kernel,
        [sheet, sheet, ((frames, 2 * width), F32), edge, edge, wide_sheet],
        (place, mask_row, q_own, k_own, v_own, kv_prev, kv_next, *grad_parts, w_out),
        smem=(0,),
        scratch=[
            pltpu.VMEM((span, width), BF16),
            pltpu.VMEM((span, width), BF16),
            pltpu.VMEM((LANES, span), BF16),
            pltpu.VMEM((LANES, span), BF16),
            pltpu.VMEM((frames, width), BF16),
            pltpu.VMEM((frames // WINDOW, 3 * WINDOW, WINDOW), F32),
            pltpu.VMEM((span, width), F32),
            pltpu.VMEM((span, width), F32),
        ],
    )
    from_next, from_prev = to_previous(edge_low), to_next(edge_high)
    held = pltpu.VMEM((2, frames, width), F32)

    def pieces(count, dtype=BF16):
        return ((count, 48, width), dtype)

    small = ((8, width), F32)
    send, keep, gain_sums = call(
        first_weights_kernel,
        [pieces(32), pieces(32), ((4, frames, LANES), F32)],
        (place, gated, attended, q_grad, normed, weights),
        smem=(0,),
        scratch=[held],
        cost=12 * square,
    )
    received = swapped(send, "core", 1)
    (branches,) = call(branch_kernel, [wide_sheet], (attended, w_out), cost=4 * square)
    branches, from_prev, from_next, received = lax.optimization_barrier(
        (branches, from_prev, from_next, received)
    )
    send2, keep2, k_grad, v_grad, gain_part = call(
        second_weights_kernel,
        [pieces(33), pieces(32), sheet, sheet, small],
        (place, kv_grad, from_prev, from_next, normed, weights, gain_sums, gain),
        smem=(0,),
        scratch=[held],
    )
    received2 = swapped(send2, "core", 1)
    near1, keep1 = call(
        first_core_kernel,
        [pieces(16), pieces(16, F32)],
        (place, keep, received),
        smem=(0,),
        vmem=16,
    )
    k_grad, near1 = lax.optimization_barrier((k_grad, near1))
    near1 = swapped(near1, "z", 1)
    exchanged = [None] * 4
    exchanged[:] = call(
        norm_kernel,
        [((2 * frames + 16, width), BF16)] * 4,
        (place, branches, q_grad, k_grad, v_grad, weights, normed, gain),
        smem=(0,),
    )
    received2, exchanged[0] = lax.optimization_barrier((received2, exchanged[0]))
    own2, *parts2, gain_part = call(
        second_core_kernel,
        [pieces(8, F32)] + [pieces(9)] * 3 + [small],
        (place, keep2, received2, gain_part),
        smem=(0,),
        vmem=16,
    )
    received2 = [shifted(part, "x", by + 1) for by, part in enumerate(parts2)]
    own1, *parts1 = call(
        first_near_kernel,
        [pieces(4, F32)] + [pieces(4)] * 3,
        (place, keep1, near1),
        smem=(0,),
        vmem=16,
    )
    received1 = [shifted(part, "x", by + 1) for by, part in enumerate(parts1)]
    exchanged[1:], received2 = lax.optimization_barrier((exchanged[1:], received2))
    exchanged[1:] = [shifted(part, "tp", by + 1) for by, part in enumerate(exchanged[1:])]
    send, keep, gain_part = call(
        second_x_kernel,
        [((208, width), BF16), ((192, width), F32), small],
        (place, own2, *received2, gain_part),
        smem=(0,),
        vmem=16,
    )
    received = swapped(send, "z", 1)
    own, *parts, gain_part = call(
        near_sum_kernel,
        [((96, width), F32)] + [((112, width), BF16)] * 3 + [small],
        (place, own1, *received1, keep, received, gain_part),
        smem=(0,),
        vmem=16,
    )
    received = [shifted(part, "z", 2 * (by + 1)) for by, part in enumerate(parts)]
    (layer_out,) = call(layer_kernel, [sheet], (tokens, mask_row, *exchanged), vmem=16)
    (tokens_grad,) = call(
        tokens_kernel,
        [sheet],
        (place, gain, tokens, out_grad, stats, *exchanged),
        smem=(0,),
        vmem=16,
    )
    received[2], layer_out, tokens_grad = lax.optimization_barrier(
        (received[2], layer_out, tokens_grad)
    )
    out_weight_grad, qkv_grad, gain_part = call(
        far_sum_kernel,
        [((24, width), F32), ((3, 24, width), F32), ((4, width), F32)],
        (own, *received, gain_part),
        vmem=16,
    )
    around = [shifted(gain_part, "tp", by) for by in (1, 2, 3)]
    gain_grad = (gain_part + around[1]) + (around[0] + around[2])
    return (
        layer_out,
        tokens_grad,
        gain_grad.reshape(-1),
        jnp.transpose(qkv_grad, (1, 0, 2)),
        out_weight_grad,
    )


def solution(mesh):
    split = Mesh(mesh.devices.reshape(8, 4, 2, 4), ("z", "x", "core", "tp"))
    return jax.shard_map(
        per_device,
        mesh=split,
        in_specs=(P(TM, "tp"), P(), P(None, None, "tp"), P(None, "tp"), P(TM), P(TM, "tp")),
        out_specs=(P(TM, "tp"), P(TM, "tp"), P(), P(TM, None, "tp"), P(TM, "tp")),
        check_vma=False,
    )
```

```python
import jax
import jax.numpy as jnp
from jax import lax
from jax.experimental import pallas as pl
from jax.experimental.pallas import tpu as pltpu
from jax.sharding import Mesh, PartitionSpec as P

HEAD = 64
WINDOW = 128
EPSILON = 1e-05
LANES = 128
TM = ("z", "x", "core")
F32 = jnp.float32
BF16 = jnp.bfloat16


def shifted(value, axis, by):
    size = lax.axis_size(axis)
    return lax.ppermute(value, axis, [(i, (i + by) % size) for i in range(size)])


def swapped(value, axis, bit):
    size = lax.axis_size(axis)
    return lax.ppermute(value, axis, [(i, i ^ bit) for i in range(size)])


def across(value, axis):
    size = lax.axis_size(axis)
    return lax.ppermute(value, axis, [(i, (i + 2 * (i % 2) - 1) % size) for i in range(size)])


def to_next(value):
    size = lax.axis_size(TM)
    return lax.ppermute(value, TM, [(i, i + 1) for i in range(size - 1)])


def to_previous(value):
    size = lax.axis_size(TM)
    return lax.ppermute(value, TM, [(i + 1, i) for i in range(size - 1)])


def dot_nn(a, b):
    return lax.dot_general(a, b, (((1,), (0,)), ((), ())), preferred_element_type=F32)


def dot_nt(a, b):
    return lax.dot_general(a, b, (((1,), (1,)), ((), ())), preferred_element_type=F32)


def dot_tn(a, b):
    return lax.dot_general(a, b, (((0,), (0,)), ((), ())), preferred_element_type=F32)


def call(body, outs, args, smem=(), far=(), scratch=(), cost=0, vmem=24):
    in_specs = [
        pl.BlockSpec(
            memory_space=pltpu.SMEM if k in smem else pltpu.HBM if k in far else pltpu.VMEM
        )
        for k in range(len(args))
    ]
    return pl.pallas_call(
        body,
        out_shape=[jax.ShapeDtypeStruct(s, d) for s, d in outs],
        in_specs=in_specs,
        out_specs=[pl.BlockSpec(memory_space=pltpu.VMEM)] * len(outs),
        scratch_shapes=list(scratch),
        cost_estimate=pl.CostEstimate(flops=cost, bytes_accessed=0, transcendentals=0),
        compiler_params=pltpu.CompilerParams(vmem_limit_bytes=vmem * 2**20),
    )(*args)


def block_of(place, step):
    return lax.rem(place[3] + step, 4)


def preload_kernel(weights, tokens, weights_here, tokens_here, arrived):
    first = pltpu.make_async_copy(weights, weights_here, arrived.at[0])
    second = pltpu.make_async_copy(tokens, tokens_here, arrived.at[1])
    first.start()
    second.start()
    first.wait()
    second.wait()


def project_kernel(
    place, t0, t1, t2, t3, gain, weights, mask, normed, q_out, k_out, v_out, kv_low, kv_high, stats
):
    parts = (t0, t1, t2, t3)
    width = 4 * t0.shape[1]
    wide = [t[...].astype(F32) for t in parts]
    average = sum(jnp.sum(t, axis=1, keepdims=True) for t in wide) / width
    centered = [t - average for t in wide]
    variance = sum(jnp.sum(t * t, axis=1, keepdims=True) for t in centered) / width
    inverse_std = lax.rsqrt(variance + EPSILON)
    lane = lax.broadcasted_iota(jnp.int32, stats.shape, 1)
    stats[...] = jnp.where(lane == 0, average, inverse_std)
    for step in range(4):
        block = block_of(place, step)
        normed[block] = (centered[step] * inverse_std * gain[block]).astype(BF16)
    rows = t0.shape[1]
    for kind, out in enumerate((q_out, k_out, v_out)):
        total = None
        for block in range(4):
            term = dot_nn(normed[block], weights[kind, rows * block : rows * (block + 1), :])
            total = term if total is None else total + term
        out[...] = total.astype(BF16)
        if kind > 0:
            columns = slice((kind - 1) * rows, kind * rows)
            kv_low[:WINDOW, columns] = out[:WINDOW, :]
            kv_high[:WINDOW, columns] = out[out.shape[0] - WINDOW :, :]
    frames = t0.shape[0]
    for out, start in ((kv_low, 0), (kv_high, frames - WINDOW)):
        row = mask[:, start : start + WINDOW].astype(F32)
        out[WINDOW:, :LANES] = jnp.broadcast_to(row, (16, LANES)).astype(BF16)


def attention_kernel(
    place, mask, q_in, k_in, v_in, kv_prev, kv_next, g0, g1, g2, g3, w_out,
    attended, q_grad, kv_grad, kv_low, kv_high, gated,
    k_ext, v_ext, k_cross, v_cross, upstream, cap, dk_ext, dv_ext,
):
    frames, width = q_in.shape
    span = 3 * WINDOW
    blocks = frames // WINDOW
    turned = []
    for block in range(blocks + 2):
        if block == 0:
            row = kv_prev[WINDOW:, :LANES].astype(F32)[:1]
        elif block > blocks:
            row = kv_next[WINDOW:, :LANES].astype(F32)[:1]
        else:
            row = mask[:, (block - 1) * WINDOW : block * WINDOW].astype(F32)
        turned.append(jnp.transpose(jnp.broadcast_to(row, (WINDOW, WINDOW))))
    key_at = lax.broadcasted_iota(jnp.int32, (WINDOW, WINDOW), 0)
    query_at = lax.broadcasted_iota(jnp.int32, (WINDOW, WINDOW), 1)
    high, low = 3.0e38, -1e30
    for block in range(blocks):
        before = (key_at >= query_at) & (turned[block] > 0)
        inside = (key_at == query_at) | (turned[block + 1] > 0)
        after = (key_at <= query_at) & (turned[block + 2] > 0)
        for part, allowed in enumerate((before, inside, after)):
            cap[block, part * WINDOW : (part + 1) * WINDOW, :] = jnp.where(allowed, high, low)

    total = None
    for step, ref in enumerate((g0, g1, g2, g3)):
        block = block_of(place, step)
        for part in range(blocks):
            rows = slice(part * WINDOW, (part + 1) * WINDOW)
            keep = turned[part + 1]
            keep = jnp.concatenate([keep] * (width // WINDOW), axis=1)
            gated[block, rows, :] = (ref[rows, :].astype(F32) * keep).astype(BF16)
    for block in range(4):
        term = dot_nn(gated[block], w_out[width * block : width * (block + 1), :])
        total = term if total is None else total + term
    upstream[...] = total.astype(BF16)

    for ext, own, at in ((k_ext, k_in, 0), (v_ext, v_in, width)):
        ext[:WINDOW, :] = kv_prev[:WINDOW, at : at + width]
        ext[WINDOW : WINDOW + frames, :] = own[...]
        ext[WINDOW + frames :, :] = kv_next[:WINDOW, at : at + width]
    dk_ext[...] = jnp.zeros_like(dk_ext)
    dv_ext[...] = jnp.zeros_like(dv_ext)
    scaling = HEAD ** (-0.5)
    first = lax.broadcasted_iota(jnp.int32, (WINDOW, LANES), 1) < HEAD
    for pair in range(width // LANES):
        lanes = slice(pair * LANES, (pair + 1) * LANES)
        k_cross[...] = jnp.transpose(k_ext[:, lanes].astype(F32) * scaling).astype(BF16)
        v_cross[...] = jnp.transpose(v_ext[:, lanes].astype(F32)).astype(BF16)
        for block in range(blocks):
            rows = slice(block * WINDOW, (block + 1) * WINDOW)
            keys = slice(block * WINDOW, block * WINDOW + span)
            query = q_in[rows, lanes] * jnp.asarray(scaling, BF16)
            zero = jnp.zeros_like(query)
            query = jnp.concatenate(
                [jnp.where(first, query, zero), jnp.where(first, zero, query)], axis=0
            )
            grad = upstream[rows, lanes]
            grad = jnp.concatenate(
                [jnp.where(first, grad, zero), jnp.where(first, zero, grad)], axis=0
            )
            bound = cap[block]
            bound = jnp.concatenate([bound, bound], axis=1)
            scores = jnp.minimum(dot_nt(k_ext[keys, lanes], query), bound)
            largest = jnp.max(scores, axis=0, keepdims=True)
            exponent = jnp.exp(scores - largest)
            probability = exponent * (1.0 / jnp.sum(exponent, axis=0, keepdims=True))
            probability_low = probability.astype(BF16)
            probability_grad = dot_nt(v_ext[keys, lanes], grad)
            row_dots = jnp.sum(probability * probability_grad, axis=0, keepdims=True)
            score_grad = (probability * (probability_grad - row_dots)).astype(BF16)
            dv_ext[keys, lanes] += dot_nn(probability_low, grad)
            dk_ext[keys, lanes] += dot_nn(score_grad, query)
            for cross, factor, out in (
                (v_cross, probability_low, attended),
                (k_cross, score_grad, q_grad),
            ):
                both = dot_nn(cross[:, keys], factor)
                both = jnp.concatenate([both[:HEAD, :WINDOW], both[HEAD:, WINDOW:]], axis=0)
                out[rows, lanes] = jnp.transpose(both).astype(BF16)
    for ext, at in ((dk_ext, 0), (dv_ext, width)):
        columns = slice(at, at + width)
        kv_low[:, columns] = ext[:WINDOW, :].astype(BF16)
        kv_grad[:, columns] = ext[WINDOW : WINDOW + frames, :]
        kv_high[:, columns] = ext[WINDOW + frames :, :].astype(BF16)


def split_rows(place, block, held, send, keep):
    core = place[2]
    for group in range(8):
        at = group % 4 * 8 + 2 * block + group // 4
        for out, whose in ((send, 1 - core), (keep, core)):
            start = pl.multiple_of(48 * group + 24 * whose, 8)
            both = jnp.concatenate([held[0, pl.ds(start, 24), :], held[1, pl.ds(start, 24), :]], 0)
            out[at] = both.astype(BF16)


def folded(value):
    return value[:, :LANES] + value[:, LANES : 2 * LANES] + value[:, 2 * LANES :]


def in_two(value):
    head = value.astype(BF16).astype(F32)
    return jnp.concatenate([head, value - head], axis=0).astype(BF16)


def from_two(value):
    wide = value.astype(F32)
    return wide[:8] + wide[8:16]


def first_weights_kernel(
    place, gated, attended, q_grad, normed, weights, send, keep, gain_sums, held
):
    width = attended.shape[1]
    for block in range(4):
        rows = slice(width * block, width * (block + 1))
        held[0] = dot_tn(gated[block], attended[...])
        held[1] = dot_tn(normed[block], q_grad[...])
        gain_sums[block] = folded(held[1] * weights[0, rows, :].astype(F32))
        split_rows(place, block, held, send, keep)


def branch_kernel(attended, w_out, branches):
    width = attended.shape[1]
    for block in range(4):
        rows = w_out[width * block : width * (block + 1), :]
        branches[block] = dot_nt(attended[...], rows).astype(BF16)


def second_weights_kernel(
    place, kv_grad, from_prev, from_next, normed, weights, gain_sums, gain,
    send, keep, k_grad, v_grad, gain_part, held,
):
    frames, width = k_grad.shape
    for out, at in ((k_grad, 0), (v_grad, width)):
        columns = slice(at, at + width)
        out[:WINDOW, :] = (
            kv_grad[:WINDOW, columns] + from_prev[:, columns].astype(F32)
        ).astype(BF16)
        out[WINDOW : frames - WINDOW, :] = kv_grad[WINDOW : frames - WINDOW, columns].astype(BF16)
        out[frames - WINDOW :, :] = (
            kv_grad[frames - WINDOW :, columns] + from_next[:, columns].astype(F32)
        ).astype(BF16)
    gain_part[...] = jnp.zeros_like(gain_part)
    for block in range(4):
        rows = slice(width * block, width * (block + 1))
        held[0] = dot_tn(normed[block], k_grad[...])
        held[1] = dot_tn(normed[block], v_grad[...])
        sums = gain_sums[block] + folded(
            held[0] * weights[1, rows, :].astype(F32) + held[1] * weights[2, rows, :].astype(F32)
        )
        for part in range(width // LANES):
            lanes = slice(part * LANES, (part + 1) * LANES)
            turned = jnp.transpose(sums[lanes, :])
            row = jnp.sum(turned, axis=0, keepdims=True)
            gain_part[block : block + 1, lanes] = row / gain[block][:, lanes]
        split_rows(place, block, held, send, keep)
    send[32, :16, :] = in_two(gain_part[...])


def norm_kernel(
    place, branches, q_grad, k_grad, v_grad, weights, normed, gain, n0, n1, n2, n3
):
    frames, width = q_grad.shape
    first_sum = second_sum = None
    for step, out in enumerate((n0, n1, n2, n3)):
        block = block_of(place, step)
        rows = pl.ds(pl.multiple_of(width * block, width), width)
        total = None
        for kind, part in enumerate((q_grad, k_grad, v_grad)):
            term = dot_nt(part[...], weights[kind, rows, :])
            total = term if total is None else total + term
        out[:frames, :] = total.astype(BF16)
        out[frames + 16 :, :] = branches[block]
        first = jnp.sum(total * gain[block], axis=1, keepdims=True)
        second = jnp.sum(total * normed[block].astype(F32), axis=1, keepdims=True)
        first_sum = first if first_sum is None else first_sum + first
        second_sum = second if second_sum is None else second_sum + second
    lane = lax.broadcasted_iota(jnp.int32, (frames, LANES), 1)
    sums = jnp.transpose(jnp.where(lane == 0, first_sum, jnp.where(lane == 1, second_sum, 0.0)))
    tail = in_two(sums[:8, :])
    for out in (n0, n1, n2, n3):
        out[frames : frames + 16, :] = tail


def tokens_kernel(place, gain, tokens, out_grad, stats, n0, n1, n2, n3, out):
    frames = tokens.shape[0]
    width = 4 * tokens.shape[1]
    average, inverse_std = stats[:, 0:1], stats[:, 1:2]
    total, rows = None, None
    for ref in (n0, n1, n2, n3):
        part = ref[:frames, :].astype(F32)
        tail = from_two(ref[frames : frames + 16, :])
        total = part if total is None else total + part
        rows = tail if rows is None else rows + tail
    rows = jnp.concatenate([rows, jnp.zeros((LANES - 8, frames), F32)], axis=0) / width
    turned = jnp.transpose(rows)
    first_mean, second_mean = turned[:, 0:1], turned[:, 1:2]
    whitened = (tokens[...].astype(F32) - average) * inverse_std
    unit = total * gain[place[3]]
    moved = (unit - first_mean - whitened * second_mean) * inverse_std
    out[...] = (out_grad[...].astype(F32) + moved).astype(BF16)


def layer_kernel(tokens, mask, n0, n1, n2, n3, out):
    total = None
    for ref in (n0, n1, n2, n3):
        term = ref[tokens.shape[0] + 16 :, :].astype(F32)
        total = term if total is None else total + term
    for part in range(tokens.shape[0] // WINDOW):
        rows = slice(part * WINDOW, (part + 1) * WINDOW)
        row = mask[:, rows].astype(F32)
        keep = jnp.transpose(jnp.broadcast_to(row, (WINDOW, WINDOW)))
        keep = jnp.concatenate([keep] * (tokens.shape[1] // WINDOW), axis=1)
        out[rows, :] = (tokens[rows, :].astype(F32) + keep * total[rows, :]).astype(BF16)


def core_sum(place, keep, received, send, own):
    parity = lax.rem(place[0], 2)
    for out, whose in ((send, 1 - parity), (own, parity)):
        for x in range(4):
            for far in range(4):
                which = 8 * x + 2 * far + whose
                total = keep[which].astype(F32) + received[which].astype(F32)
                out[4 * x + far] = total.astype(out.dtype)


def first_core_kernel(place, keep, received, send, own):
    core_sum(place, keep, received, send, own)


def gain_kernel(received, gain_part, gain_sum):
    gain_sum[...] = from_two(in_two(gain_part[...])) + from_two(received[32, :16, :])


def second_core_kernel(place, keep, received, g0, g1, g2, g3, send, own, gain_sum):
    core_sum(place, keep, received, send, own)
    gain_sum[...] = (g0[...] + g2[...]) + (g1[...] + g3[...])
    send[16, :16, :] = in_two(gain_sum[...])


def first_near_kernel(keep, received, total):
    for which in range(16):
        total[which] = keep[which] + received[which].astype(F32)


def near_kernel(place, sum1, keep, received, gain_part, own, p1, p2, p3, gain_sum):
    gain_sum[...] = from_two(in_two(gain_part[...])) + from_two(received[16, :16, :])
    for step, out in enumerate((own, p1, p2, p3)):
        for far in range(4):
            which = lax.rem(place[1] + step, 4) * 4 + far
            out[96 * far : 96 * far + 48, :] = sum1[which].astype(out.dtype)
            total = keep[which] + received[which].astype(F32)
            out[96 * far + 48 : 96 * far + 96, :] = total.astype(out.dtype)
        if step:
            out[384:, :] = in_two(gain_sum[...])


def x_sum_kernel(place, kept, r1, r2, r3, gain_part, own, p1, p2, p3, gain_sum):
    near = from_two(in_two(gain_part[...])) + from_two(r2[384:, :])
    gain_sum[...] = near + (from_two(r1[384:, :]) + from_two(r3[384:, :]))
    for step, out in enumerate((own, p1, p2, p3)):
        far = lax.rem(lax.div(place[0], 2) + step, 4)
        rows = pl.ds(pl.multiple_of(96 * far, 32), 96)
        total = kept[rows, :] + r2[rows, :].astype(F32)
        total = total + (r1[rows, :].astype(F32) + r3[rows, :].astype(F32))
        out[:96, :] = total.astype(out.dtype)
        if step:
            out[96:, :] = in_two(gain_sum[...])


def far_sum_kernel(own, r1, r2, r3, gain_part, out_weight, qkv_weight, gain_sum):
    total = own[...] + r2[:96, :].astype(F32)
    total = total + (r1[:96, :].astype(F32) + r3[:96, :].astype(F32))
    out_weight[...] = total[:24]
    for kind in range(3):
        qkv_weight[kind] = total[24 * (kind + 1) : 24 * (kind + 2)]
    near = from_two(in_two(gain_part[...])) + from_two(r2[96:, :])
    gain_sum[...] = (near + (from_two(r1[96:, :]) + from_two(r3[96:, :])))[:4]


def per_device(tokens, ln_gain, w_qkv, w_out, frame_mask, out_grad):
    frames, width = tokens.shape
    place = jnp.stack([lax.axis_index(a) for a in ("z", "x", "core", "tp")]).astype(jnp.int32)
    token_parts = [tokens] + [shifted(tokens, "tp", -step) for step in (1, 2, 3)]
    late, token_parts[3] = lax.optimization_barrier((out_grad, token_parts[3]))
    grad_parts = [out_grad] + [shifted(late, "tp", -step) for step in (1, 2, 3)]
    mask_row = frame_mask[None, :]
    gain = ln_gain.reshape(4, 1, width)
    weights = jnp.transpose(w_qkv, (1, 0, 2))
    weights_here, token_parts[0] = call(
        preload_kernel,
        [(weights.shape, BF16), ((frames, width), BF16)],
        (weights, tokens),
        far=(0, 1),
        scratch=[pltpu.SemaphoreType.DMA((2,))],
        cost=2**30,
        vmem=8,
    )

    sheet, wide_sheet = ((frames, width), BF16), ((4, frames, width), BF16)
    edge, halo = ((WINDOW, 2 * width), BF16), ((WINDOW + 16, 2 * width), BF16)
    square = frames * width * width * 2
    normed, q_own, k_own, v_own, kv_low, kv_high, stats = call(
        project_kernel,
        [wide_sheet, sheet, sheet, sheet, halo, halo, ((frames, LANES), F32)],
        (place, *token_parts, gain, weights_here, mask_row),
        smem=(0,),
        cost=12 * square,
    )
    kv_prev, kv_next = to_next(kv_high), to_previous(kv_low)
    span = frames + 2 * WINDOW
    attended, q_grad, kv_grad, edge_low, edge_high, gated = call(
        attention_kernel,
        [sheet, sheet, ((frames, 2 * width), F32), edge, edge, wide_sheet],
        (place, mask_row, q_own, k_own, v_own, kv_prev, kv_next, *grad_parts, w_out),
        smem=(0,),
        scratch=[
            pltpu.VMEM((span, width), BF16),
            pltpu.VMEM((span, width), BF16),
            pltpu.VMEM((LANES, span), BF16),
            pltpu.VMEM((LANES, span), BF16),
            pltpu.VMEM((frames, width), BF16),
            pltpu.VMEM((frames // WINDOW, 3 * WINDOW, WINDOW), F32),
            pltpu.VMEM((span, width), F32),
            pltpu.VMEM((span, width), F32),
        ],
    )
    from_next, from_prev = to_previous(edge_low), to_next(edge_high)
    held = pltpu.VMEM((2, frames, width), F32)

    def pieces(count, dtype=BF16):
        return ((count, 48, width), dtype)

    small = ((8, width), F32)
    send, keep, gain_sums = call(
        first_weights_kernel,
        [pieces(32), pieces(32), ((4, frames, LANES), F32)],
        (place, gated, attended, q_grad, normed, weights),
        smem=(0,),
        scratch=[held],
        cost=12 * square,
    )
    received = swapped(send, "core", 1)
    (branches,) = call(branch_kernel, [wide_sheet], (attended, w_out), cost=4 * square)
    branches, from_prev, from_next, received = lax.optimization_barrier(
        (branches, from_prev, from_next, received)
    )
    send2, keep2, k_grad, v_grad, gain_part = call(
        second_weights_kernel,
        [pieces(33), pieces(32), sheet, sheet, small],
        (place, kv_grad, from_prev, from_next, normed, weights, gain_sums, gain),
        smem=(0,),
        scratch=[held],
    )
    received2 = swapped(send2, "core", 1)
    near1, keep1 = call(
        first_core_kernel,
        [pieces(16), pieces(16, F32)],
        (place, keep, received),
        smem=(0,),
        vmem=16,
    )
    k_grad, near1 = lax.optimization_barrier((k_grad, near1))
    near1 = swapped(near1, "z", 1)
    exchanged = call(
        norm_kernel,
        [((2 * frames + 16, width), BF16)] * 4,
        (place, branches, q_grad, k_grad, v_grad, weights, normed, gain),
        smem=(0,),
    )
    exchanged = list(exchanged)
    received2, exchanged[0] = lax.optimization_barrier((received2, exchanged[0]))
    (gain_part,) = call(gain_kernel, [small], (received2, gain_part), vmem=8)
    gains = [gain_part] + [shifted(gain_part, "tp", by) for by in (1, 2, 3)]
    near2, keep2, gain_part = call(
        second_core_kernel,
        [pieces(17), pieces(16, F32), small],
        (place, keep2, received2, *gains),
        smem=(0,),
        vmem=16,
    )
    near2 = across(near2, "z")
    (sum1,) = call(first_near_kernel, [pieces(16, F32)], (keep1, near1), vmem=16)
    exchanged, gain_part = lax.optimization_barrier((exchanged, gain_part))
    exchanged = list(exchanged)
    exchanged[1:] = [shifted(part, "tp", by + 1) for by, part in enumerate(exchanged[1:])]
    own, *parts, gain_part = call(
        near_kernel,
        [((384, width), F32)] + [((400, width), BF16)] * 3 + [small],
        (place, sum1, keep2, near2, gain_part),
        smem=(0,),
        vmem=16,
    )
    received = [shifted(part, "x", by + 1) for by, part in enumerate(parts)]
    own, *parts, gain_part = call(
        x_sum_kernel,
        [((96, width), F32)] + [((112, width), BF16)] * 3 + [small],
        (place, own, *received, gain_part),
        smem=(0,),
        vmem=16,
    )
    received = [shifted(part, "z", 2 * (by + 1)) for by, part in enumerate(parts)]
    (layer_out,) = call(layer_kernel, [sheet], (tokens, mask_row, *exchanged), vmem=16)
    (tokens_grad,) = call(
        tokens_kernel,
        [sheet],
        (place, gain, tokens, out_grad, stats, *exchanged),
        smem=(0,),
        vmem=16,
    )
    received[2], layer_out, tokens_grad = lax.optimization_barrier(
        (received[2], layer_out, tokens_grad)
    )
    out_weight_grad, qkv_grad, gain_grad = call(
        far_sum_kernel,
        [((24, width), F32), ((3, 24, width), F32), ((4, width), F32)],
        (own, *received, gain_part),
        vmem=16,
    )
    return (
        layer_out,
        tokens_grad,
        gain_grad.reshape(-1),
        jnp.transpose(qkv_grad, (1, 0, 2)),
        out_weight_grad,
    )


def solution(mesh):
    split = Mesh(mesh.devices.reshape(8, 4, 2, 4), ("z", "x", "core", "tp"))
    return jax.shard_map(
        per_device,
        mesh=split,
        in_specs=(P(TM, "tp"), P(), P(None, None, "tp"), P(None, "tp"), P(TM), P(TM, "tp")),
        out_specs=(P(TM, "tp"), P(TM, "tp"), P(), P(TM, None, "tp"), P(TM, "tp")),
        check_vma=False,
    )
```

```python
import jax
import jax.numpy as jnp
from jax import lax
from jax.experimental import pallas as pl
from jax.experimental.pallas import tpu as pltpu
from jax.sharding import Mesh, PartitionSpec as P

HEAD = 64
WINDOW = 128
EPSILON = 1e-05
LANES = 128
TM = ("z", "x", "core")
F32 = jnp.float32
BF16 = jnp.bfloat16


def shifted(value, axis, by):
    size = lax.axis_size(axis)
    return lax.ppermute(value, axis, [(i, (i + by) % size) for i in range(size)])


def swapped(value, axis, bit):
    size = lax.axis_size(axis)
    return lax.ppermute(value, axis, [(i, i ^ bit) for i in range(size)])


def across(value, axis):
    size = lax.axis_size(axis)
    return lax.ppermute(value, axis, [(i, (i + 2 * (i % 2) - 1) % size) for i in range(size)])


def to_next(value):
    size = lax.axis_size(TM)
    return lax.ppermute(value, TM, [(i, i + 1) for i in range(size - 1)])


def to_previous(value):
    size = lax.axis_size(TM)
    return lax.ppermute(value, TM, [(i + 1, i) for i in range(size - 1)])


def dot_nn(a, b):
    return lax.dot_general(a, b, (((1,), (0,)), ((), ())), preferred_element_type=F32)


def dot_nt(a, b):
    return lax.dot_general(a, b, (((1,), (1,)), ((), ())), preferred_element_type=F32)


def dot_tn(a, b):
    return lax.dot_general(a, b, (((0,), (0,)), ((), ())), preferred_element_type=F32)


def call(body, outs, args, smem=(), far=(), scratch=(), cost=0, vmem=24):
    in_specs = [
        pl.BlockSpec(
            memory_space=pltpu.SMEM if k in smem else pltpu.HBM if k in far else pltpu.VMEM
        )
        for k in range(len(args))
    ]
    return pl.pallas_call(
        body,
        out_shape=[jax.ShapeDtypeStruct(s, d) for s, d in outs],
        in_specs=in_specs,
        out_specs=[pl.BlockSpec(memory_space=pltpu.VMEM)] * len(outs),
        scratch_shapes=list(scratch),
        cost_estimate=pl.CostEstimate(flops=cost, bytes_accessed=0, transcendentals=0),
        compiler_params=pltpu.CompilerParams(vmem_limit_bytes=vmem * 2**20),
    )(*args)


def block_of(place, step):
    return lax.rem(place[3] + step, 4)


def preload_kernel(weights, tokens, weights_here, tokens_here, arrived):
    first = pltpu.make_async_copy(weights, weights_here, arrived.at[0])
    second = pltpu.make_async_copy(tokens, tokens_here, arrived.at[1])
    first.start()
    second.start()
    first.wait()
    second.wait()


def project_kernel(
    place, t0, t1, t2, t3, gain, weights, mask, normed, q_out, k_out, v_out, kv_low, kv_high, stats
):
    parts = (t0, t1, t2, t3)
    width = 4 * t0.shape[1]
    wide = [t[...].astype(F32) for t in parts]
    average = sum(jnp.sum(t, axis=1, keepdims=True) for t in wide) / width
    centered = [t - average for t in wide]
    variance = sum(jnp.sum(t * t, axis=1, keepdims=True) for t in centered) / width
    inverse_std = lax.rsqrt(variance + EPSILON)
    lane = lax.broadcasted_iota(jnp.int32, stats.shape, 1)
    stats[...] = jnp.where(lane == 0, average, inverse_std)
    for step in range(4):
        block = block_of(place, step)
        normed[block] = (centered[step] * inverse_std * gain[block]).astype(BF16)
    rows = t0.shape[1]
    for kind, out in enumerate((q_out, k_out, v_out)):
        total = None
        for block in range(4):
            term = dot_nn(normed[block], weights[kind, rows * block : rows * (block + 1), :])
            total = term if total is None else total + term
        out[...] = total.astype(BF16)
        if kind > 0:
            columns = slice((kind - 1) * rows, kind * rows)
            kv_low[:WINDOW, columns] = out[:WINDOW, :]
            kv_high[:WINDOW, columns] = out[out.shape[0] - WINDOW :, :]
    frames = t0.shape[0]
    for out, start in ((kv_low, 0), (kv_high, frames - WINDOW)):
        row = mask[:, start : start + WINDOW].astype(F32)
        out[WINDOW:, :LANES] = jnp.broadcast_to(row, (16, LANES)).astype(BF16)


def attention_kernel(
    place, mask, q_in, k_in, v_in, kv_prev, kv_next, g0, g1, g2, g3, w_out,
    attended, q_grad, kv_grad, kv_low, kv_high, gated,
    k_ext, v_ext, k_cross, v_cross, upstream, cap, dk_ext, dv_ext,
):
    frames, width = q_in.shape
    span = 3 * WINDOW
    blocks = frames // WINDOW
    turned = []
    for block in range(blocks + 2):
        if block == 0:
            row = kv_prev[WINDOW:, :LANES].astype(F32)[:1]
        elif block > blocks:
            row = kv_next[WINDOW:, :LANES].astype(F32)[:1]
        else:
            row = mask[:, (block - 1) * WINDOW : block * WINDOW].astype(F32)
        turned.append(jnp.transpose(jnp.broadcast_to(row, (WINDOW, WINDOW))))
    key_at = lax.broadcasted_iota(jnp.int32, (WINDOW, WINDOW), 0)
    query_at = lax.broadcasted_iota(jnp.int32, (WINDOW, WINDOW), 1)
    high, low = 3.0e38, -1e30
    for block in range(blocks):
        before = (key_at >= query_at) & (turned[block] > 0)
        inside = (key_at == query_at) | (turned[block + 1] > 0)
        after = (key_at <= query_at) & (turned[block + 2] > 0)
        for part, allowed in enumerate((before, inside, after)):
            cap[block, part * WINDOW : (part + 1) * WINDOW, :] = jnp.where(allowed, high, low)

    total = None
    for step, ref in enumerate((g0, g1, g2, g3)):
        block = block_of(place, step)
        for part in range(blocks):
            rows = slice(part * WINDOW, (part + 1) * WINDOW)
            keep = turned[part + 1]
            keep = jnp.concatenate([keep] * (width // WINDOW), axis=1)
            gated[block, rows, :] = (ref[rows, :].astype(F32) * keep).astype(BF16)
    for block in range(4):
        term = dot_nn(gated[block], w_out[width * block : width * (block + 1), :])
        total = term if total is None else total + term
    upstream[...] = total.astype(BF16)

    for ext, own, at in ((k_ext, k_in, 0), (v_ext, v_in, width)):
        ext[:WINDOW, :] = kv_prev[:WINDOW, at : at + width]
        ext[WINDOW : WINDOW + frames, :] = own[...]
        ext[WINDOW + frames :, :] = kv_next[:WINDOW, at : at + width]
    dk_ext[...] = jnp.zeros_like(dk_ext)
    dv_ext[...] = jnp.zeros_like(dv_ext)
    scaling = HEAD ** (-0.5)
    first = lax.broadcasted_iota(jnp.int32, (WINDOW, LANES), 1) < HEAD
    for pair in range(width // LANES):
        lanes = slice(pair * LANES, (pair + 1) * LANES)
        k_cross[...] = jnp.transpose(k_ext[:, lanes].astype(F32) * scaling).astype(BF16)
        v_cross[...] = jnp.transpose(v_ext[:, lanes].astype(F32)).astype(BF16)
        for block in range(blocks):
            rows = slice(block * WINDOW, (block + 1) * WINDOW)
            keys = slice(block * WINDOW, block * WINDOW + span)
            query = q_in[rows, lanes] * jnp.asarray(scaling, BF16)
            zero = jnp.zeros_like(query)
            query = jnp.concatenate(
                [jnp.where(first, query, zero), jnp.where(first, zero, query)], axis=0
            )
            grad = upstream[rows, lanes]
            grad = jnp.concatenate(
                [jnp.where(first, grad, zero), jnp.where(first, zero, grad)], axis=0
            )
            bound = cap[block]
            bound = jnp.concatenate([bound, bound], axis=1)
            scores = jnp.minimum(dot_nt(k_ext[keys, lanes], query), bound)
            largest = jnp.max(scores, axis=0, keepdims=True)
            exponent = jnp.exp(scores - largest)
            probability = exponent * (1.0 / jnp.sum(exponent, axis=0, keepdims=True))
            probability_low = probability.astype(BF16)
            probability_grad = dot_nt(v_ext[keys, lanes], grad)
            row_dots = jnp.sum(probability * probability_grad, axis=0, keepdims=True)
            score_grad = (probability * (probability_grad - row_dots)).astype(BF16)
            dv_ext[keys, lanes] += dot_nn(probability_low, grad)
            dk_ext[keys, lanes] += dot_nn(score_grad, query)
            for cross, factor, out in (
                (v_cross, probability_low, attended),
                (k_cross, score_grad, q_grad),
            ):
                both = dot_nn(cross[:, keys], factor)
                both = jnp.concatenate([both[:HEAD, :WINDOW], both[HEAD:, WINDOW:]], axis=0)
                out[rows, lanes] = jnp.transpose(both).astype(BF16)
    for ext, at in ((dk_ext, 0), (dv_ext, width)):
        columns = slice(at, at + width)
        kv_low[:, columns] = ext[:WINDOW, :].astype(BF16)
        kv_grad[:, columns] = ext[WINDOW : WINDOW + frames, :]
        kv_high[:, columns] = ext[WINDOW + frames :, :].astype(BF16)


def split_rows(place, block, held, send, keep):
    core = place[2]
    for group in range(8):
        at = group % 4 * 8 + 2 * block + group // 4
        for out, whose in ((send, 1 - core), (keep, core)):
            start = pl.multiple_of(48 * group + 24 * whose, 8)
            both = jnp.concatenate([held[0, pl.ds(start, 24), :], held[1, pl.ds(start, 24), :]], 0)
            out[at] = both.astype(BF16)


def folded(value):
    return value[:, :LANES] + value[:, LANES : 2 * LANES] + value[:, 2 * LANES :]


def in_two(value):
    head = value.astype(BF16).astype(F32)
    return jnp.concatenate([head, value - head], axis=0).astype(BF16)


def from_two(value):
    wide = value.astype(F32)
    return wide[:8] + wide[8:16]


def first_weights_kernel(
    place, gated, attended, q_grad, normed, weights, send, keep, gain_sums, held
):
    width = attended.shape[1]
    for block in range(4):
        rows = slice(width * block, width * (block + 1))
        held[0] = dot_tn(gated[block], attended[...])
        held[1] = dot_tn(normed[block], q_grad[...])
        gain_sums[block] = folded(held[1] * weights[0, rows, :].astype(F32))
        split_rows(place, block, held, send, keep)


def branch_kernel(attended, w_out, branches):
    width = attended.shape[1]
    for block in range(4):
        rows = w_out[width * block : width * (block + 1), :]
        branches[block] = dot_nt(attended[...], rows).astype(BF16)


def second_weights_kernel(
    place, kv_grad, from_prev, from_next, normed, weights, gain_sums, gain,
    send, keep, k_grad, v_grad, gain_part, held,
):
    frames, width = k_grad.shape
    for out, at in ((k_grad, 0), (v_grad, width)):
        columns = slice(at, at + width)
        out[:WINDOW, :] = (
            kv_grad[:WINDOW, columns] + from_prev[:, columns].astype(F32)
        ).astype(BF16)
        out[WINDOW : frames - WINDOW, :] = kv_grad[WINDOW : frames - WINDOW, columns].astype(BF16)
        out[frames - WINDOW :, :] = (
            kv_grad[frames - WINDOW :, columns] + from_next[:, columns].astype(F32)
        ).astype(BF16)
    gain_part[...] = jnp.zeros_like(gain_part)
    for block in range(4):
        rows = slice(width * block, width * (block + 1))
        held[0] = dot_tn(normed[block], k_grad[...])
        held[1] = dot_tn(normed[block], v_grad[...])
        sums = gain_sums[block] + folded(
            held[0] * weights[1, rows, :].astype(F32) + held[1] * weights[2, rows, :].astype(F32)
        )
        for part in range(width // LANES):
            lanes = slice(part * LANES, (part + 1) * LANES)
            turned = jnp.transpose(sums[lanes, :])
            row = jnp.sum(turned, axis=0, keepdims=True)
            gain_part[block : block + 1, lanes] = row / gain[block][:, lanes]
        split_rows(place, block, held, send, keep)
    send[32, :16, :] = in_two(gain_part[...])


def norm_kernel(
    place, branches, q_grad, k_grad, v_grad, weights, normed, gain, n0, n1, n2, n3
):
    frames, width = q_grad.shape
    first_sum = second_sum = None
    for step, out in enumerate((n0, n1, n2, n3)):
        block = block_of(place, step)
        rows = pl.ds(pl.multiple_of(width * block, width), width)
        total = None
        for kind, part in enumerate((q_grad, k_grad, v_grad)):
            term = dot_nt(part[...], weights[kind, rows, :])
            total = term if total is None else total + term
        out[:frames, :] = total.astype(BF16)
        out[frames + 16 :, :] = branches[block]
        first = jnp.sum(total * gain[block], axis=1, keepdims=True)
        second = jnp.sum(total * normed[block].astype(F32), axis=1, keepdims=True)
        first_sum = first if first_sum is None else first_sum + first
        second_sum = second if second_sum is None else second_sum + second
    lane = lax.broadcasted_iota(jnp.int32, (frames, LANES), 1)
    sums = jnp.transpose(jnp.where(lane == 0, first_sum, jnp.where(lane == 1, second_sum, 0.0)))
    tail = in_two(sums[:8, :])
    for out in (n0, n1, n2, n3):
        out[frames : frames + 16, :] = tail


def tokens_kernel(place, gain, tokens, out_grad, stats, n0, n1, n2, n3, out):
    frames = tokens.shape[0]
    width = 4 * tokens.shape[1]
    average, inverse_std = stats[:, 0:1], stats[:, 1:2]
    total, rows = None, None
    for ref in (n0, n1, n2, n3):
        part = ref[:frames, :].astype(F32)
        tail = from_two(ref[frames : frames + 16, :])
        total = part if total is None else total + part
        rows = tail if rows is None else rows + tail
    rows = jnp.concatenate([rows, jnp.zeros((LANES - 8, frames), F32)], axis=0) / width
    turned = jnp.transpose(rows)
    first_mean, second_mean = turned[:, 0:1], turned[:, 1:2]
    whitened = (tokens[...].astype(F32) - average) * inverse_std
    unit = total * gain[place[3]]
    moved = (unit - first_mean - whitened * second_mean) * inverse_std
    out[...] = (out_grad[...].astype(F32) + moved).astype(BF16)


def layer_kernel(tokens, mask, n0, n1, n2, n3, out):
    total = None
    for ref in (n0, n1, n2, n3):
        term = ref[tokens.shape[0] + 16 :, :].astype(F32)
        total = term if total is None else total + term
    for part in range(tokens.shape[0] // WINDOW):
        rows = slice(part * WINDOW, (part + 1) * WINDOW)
        row = mask[:, rows].astype(F32)
        keep = jnp.transpose(jnp.broadcast_to(row, (WINDOW, WINDOW)))
        keep = jnp.concatenate([keep] * (tokens.shape[1] // WINDOW), axis=1)
        out[rows, :] = (tokens[rows, :].astype(F32) + keep * total[rows, :]).astype(BF16)


def core_sum(place, keep, received, send, own):
    parity = lax.rem(place[0], 2)
    for out, whose in ((send, 1 - parity), (own, parity)):
        for x in range(4):
            for far in range(4):
                which = 8 * x + 2 * far + whose
                total = keep[which].astype(F32) + received[which].astype(F32)
                out[4 * x + far] = total.astype(out.dtype)


def first_core_kernel(place, keep, received, send, own):
    core_sum(place, keep, received, send, own)


def gain_kernel(received, gain_part, gain_sum):
    gain_sum[...] = from_two(in_two(gain_part[...])) + from_two(received[32, :16, :])


def second_core_kernel(place, keep, received, g0, g1, g2, g3, send, own, gain_sum):
    core_sum(place, keep, received, send, own)
    gain_sum[...] = (g0[...] + g2[...]) + (g1[...] + g3[...])
    send[16, :16, :] = in_two(gain_sum[...])


def first_near_kernel(keep, received, total):
    for which in range(16):
        total[which] = keep[which] + received[which].astype(F32)


def near_kernel(place, sum1, keep, received, gain_part, own, p1, p2, p3, gain_sum):
    gain_sum[...] = from_two(in_two(gain_part[...])) + from_two(received[16, :16, :])
    for step, out in enumerate((own, p1, p2, p3)):
        for far in range(4):
            which = lax.rem(place[1] + step, 4) * 4 + far
            out[96 * far : 96 * far + 48, :] = sum1[which].astype(out.dtype)
            total = keep[which] + received[which].astype(F32)
            out[96 * far + 48 : 96 * far + 96, :] = total.astype(out.dtype)
        if step:
            out[384:, :] = in_two(gain_sum[...])


def x_sum_kernel(place, kept, r1, r2, r3, gain_part, own, p1, p2, p3, gain_sum):
    near = from_two(in_two(gain_part[...])) + from_two(r2[384:, :])
    gain_sum[...] = near + (from_two(r1[384:, :]) + from_two(r3[384:, :]))
    for step, out in enumerate((own, p1, p2, p3)):
        far = lax.rem(lax.div(place[0], 2) + step, 4)
        rows = pl.ds(pl.multiple_of(96 * far, 32), 96)
        total = kept[rows, :] + r2[rows, :].astype(F32)
        total = total + (r1[rows, :].astype(F32) + r3[rows, :].astype(F32))
        out[:96, :] = total.astype(out.dtype)
        if step:
            out[96:, :] = in_two(gain_sum[...])


def far_sum_kernel(own, r1, r2, r3, gain_part, out_weight, qkv_weight, gain_sum):
    total = own[...] + r2[:96, :].astype(F32)
    total = total + (r1[:96, :].astype(F32) + r3[:96, :].astype(F32))
    out_weight[...] = total[:24]
    for kind in range(3):
        qkv_weight[kind] = total[24 * (kind + 1) : 24 * (kind + 2)]
    near = from_two(in_two(gain_part[...])) + from_two(r2[96:, :])
    gain_sum[...] = (near + (from_two(r1[96:, :]) + from_two(r3[96:, :])))[:4]


def per_device(tokens, ln_gain, w_qkv, w_out, frame_mask, out_grad):
    frames, width = tokens.shape
    place = jnp.stack([lax.axis_index(a) for a in ("z", "x", "core", "tp")]).astype(jnp.int32)
    token_parts = [tokens] + [shifted(tokens, "tp", -step) for step in (1, 2, 3)]
    late, token_parts[3] = lax.optimization_barrier((out_grad, token_parts[3]))
    grad_parts = [out_grad] + [shifted(late, "tp", -step) for step in (1, 2, 3)]
    mask_row = frame_mask[None, :]
    gain = ln_gain.reshape(4, 1, width)
    weights = jnp.transpose(w_qkv, (1, 0, 2))
    weights_here, token_parts[0] = call(
        preload_kernel,
        [(weights.shape, BF16), ((frames, width), BF16)],
        (weights, tokens),
        far=(0, 1),
        scratch=[pltpu.SemaphoreType.DMA((2,))],
        cost=2**30,
        vmem=8,
    )

    sheet, wide_sheet = ((frames, width), BF16), ((4, frames, width), BF16)
    edge, halo = ((WINDOW, 2 * width), BF16), ((WINDOW + 16, 2 * width), BF16)
    square = frames * width * width * 2
    normed, q_own, k_own, v_own, kv_low, kv_high, stats = call(
        project_kernel,
        [wide_sheet, sheet, sheet, sheet, halo, halo, ((frames, LANES), F32)],
        (place, *token_parts, gain, weights_here, mask_row),
        smem=(0,),
        cost=12 * square,
    )
    kv_prev, kv_next = to_next(kv_high), to_previous(kv_low)
    span = frames + 2 * WINDOW
    attended, q_grad, kv_grad, edge_low, edge_high, gated = call(
        attention_kernel,
        [sheet, sheet, ((frames, 2 * width), F32), edge, edge, wide_sheet],
        (place, mask_row, q_own, k_own, v_own, kv_prev, kv_next, *grad_parts, w_out),
        smem=(0,),
        scratch=[
            pltpu.VMEM((span, width), BF16),
            pltpu.VMEM((span, width), BF16),
            pltpu.VMEM((LANES, span), BF16),
            pltpu.VMEM((LANES, span), BF16),
            pltpu.VMEM((frames, width), BF16),
            pltpu.VMEM((frames // WINDOW, 3 * WINDOW, WINDOW), F32),
            pltpu.VMEM((span, width), F32),
            pltpu.VMEM((span, width), F32),
        ],
    )
    from_next, from_prev = to_previous(edge_low), to_next(edge_high)
    held = pltpu.VMEM((2, frames, width), F32)

    def pieces(count, dtype=BF16):
        return ((count, 48, width), dtype)

    small = ((8, width), F32)
    send, keep, gain_sums = call(
        first_weights_kernel,
        [pieces(32), pieces(32), ((4, frames, LANES), F32)],
        (place, gated, attended, q_grad, normed, weights),
        smem=(0,),
        scratch=[held],
        cost=12 * square,
    )
    received = swapped(send, "core", 1)
    (branches,) = call(branch_kernel, [wide_sheet], (attended, w_out), cost=4 * square)
    branches, from_prev, from_next, received = lax.optimization_barrier(
        (branches, from_prev, from_next, received)
    )
    send2, keep2, k_grad, v_grad, gain_part = call(
        second_weights_kernel,
        [pieces(33), pieces(32), sheet, sheet, small],
        (place, kv_grad, from_prev, from_next, normed, weights, gain_sums, gain),
        smem=(0,),
        scratch=[held],
    )
    received2 = swapped(send2, "core", 1)
    near1, keep1 = call(
        first_core_kernel,
        [pieces(16), pieces(16, F32)],
        (place, keep, received),
        smem=(0,),
        vmem=16,
    )
    k_grad, near1 = lax.optimization_barrier((k_grad, near1))
    near1 = swapped(near1, "z", 1)
    exchanged = call(
        norm_kernel,
        [((2 * frames + 16, width), BF16)] * 4,
        (place, branches, q_grad, k_grad, v_grad, weights, normed, gain),
        smem=(0,),
    )
    exchanged = list(exchanged)
    received2, exchanged[0] = lax.optimization_barrier((received2, exchanged[0]))
    (gain_part,) = call(gain_kernel, [small], (received2, gain_part), vmem=8)
    gains = [gain_part] + [shifted(gain_part, "tp", by) for by in (1, 2, 3)]
    near2, keep2, gain_part = call(
        second_core_kernel,
        [pieces(17), pieces(16, F32), small],
        (place, keep2, received2, *gains),
        smem=(0,),
        vmem=16,
    )
    near2 = across(near2, "z")
    (sum1,) = call(first_near_kernel, [pieces(16, F32)], (keep1, near1), vmem=16)
    exchanged, gain_part = lax.optimization_barrier((exchanged, gain_part))
    exchanged = list(exchanged)
    exchanged[1:] = [shifted(part, "tp", by + 1) for by, part in enumerate(exchanged[1:])]
    own, *parts, gain_part = call(
        near_kernel,
        [((384, width), F32)] + [((400, width), BF16)] * 3 + [small],
        (place, sum1, keep2, near2, gain_part),
        smem=(0,),
        vmem=16,
    )
    received = [shifted(part, "x", by + 1) for by, part in enumerate(parts)]
    received[2], exchanged[2] = lax.optimization_barrier((received[2], exchanged[2]))
    own, *parts, gain_part = call(
        x_sum_kernel,
        [((96, width), F32)] + [((112, width), BF16)] * 3 + [small],
        (place, own, *received, gain_part),
        smem=(0,),
        vmem=16,
    )
    received = [shifted(part, "z", 2 * (by + 1)) for by, part in enumerate(parts)]
    (layer_out,) = call(layer_kernel, [sheet], (tokens, mask_row, *exchanged), vmem=16)
    (tokens_grad,) = call(
        tokens_kernel,
        [sheet],
        (place, gain, tokens, out_grad, stats, *exchanged),
        smem=(0,),
        vmem=16,
    )
    received[2], layer_out, tokens_grad = lax.optimization_barrier(
        (received[2], layer_out, tokens_grad)
    )
    out_weight_grad, qkv_grad, gain_grad = call(
        far_sum_kernel,
        [((24, width), F32), ((3, 24, width), F32), ((4, width), F32)],
        (own, *received, gain_part),
        vmem=16,
    )
    return (
        layer_out,
        tokens_grad,
        gain_grad.reshape(-1),
        jnp.transpose(qkv_grad, (1, 0, 2)),
        out_weight_grad,
    )


def solution(mesh):
    split = Mesh(mesh.devices.reshape(8, 4, 2, 4), ("z", "x", "core", "tp"))
    return jax.shard_map(
        per_device,
        mesh=split,
        in_specs=(P(TM, "tp"), P(), P(None, None, "tp"), P(None, "tp"), P(TM), P(TM, "tp")),
        out_specs=(P(TM, "tp"), P(TM, "tp"), P(), P(TM, None, "tp"), P(TM, "tp")),
        check_vma=False,
    )
```

```python
import jax
import jax.numpy as jnp
from jax import lax
from jax.experimental import pallas as pl
from jax.experimental.pallas import tpu as pltpu
from jax.sharding import Mesh, PartitionSpec as P

HEAD = 64
WINDOW = 128
EPSILON = 1e-05
LANES = 128
TM = ("z", "x", "core")
F32 = jnp.float32
BF16 = jnp.bfloat16


def shifted(value, axis, by):
    size = lax.axis_size(axis)
    return lax.ppermute(value, axis, [(i, (i + by) % size) for i in range(size)])


def swapped(value, axis, bit):
    size = lax.axis_size(axis)
    return lax.ppermute(value, axis, [(i, i ^ bit) for i in range(size)])


def across(value, axis):
    size = lax.axis_size(axis)
    return lax.ppermute(value, axis, [(i, (i + 2 * (i % 2) - 1) % size) for i in range(size)])


def to_next(value):
    size = lax.axis_size(TM)
    return lax.ppermute(value, TM, [(i, i + 1) for i in range(size - 1)])


def to_previous(value):
    size = lax.axis_size(TM)
    return lax.ppermute(value, TM, [(i + 1, i) for i in range(size - 1)])


def dot_nn(a, b):
    return lax.dot_general(a, b, (((1,), (0,)), ((), ())), preferred_element_type=F32)


def dot_nt(a, b):
    return lax.dot_general(a, b, (((1,), (1,)), ((), ())), preferred_element_type=F32)


def dot_tn(a, b):
    return lax.dot_general(a, b, (((0,), (0,)), ((), ())), preferred_element_type=F32)


def call(body, outs, args, smem=(), far=(), scratch=(), cost=0, vmem=24):
    in_specs = [
        pl.BlockSpec(
            memory_space=pltpu.SMEM if k in smem else pltpu.HBM if k in far else pltpu.VMEM
        )
        for k in range(len(args))
    ]
    return pl.pallas_call(
        body,
        out_shape=[jax.ShapeDtypeStruct(s, d) for s, d in outs],
        in_specs=in_specs,
        out_specs=[pl.BlockSpec(memory_space=pltpu.VMEM)] * len(outs),
        scratch_shapes=list(scratch),
        cost_estimate=pl.CostEstimate(flops=cost, bytes_accessed=0, transcendentals=0),
        compiler_params=pltpu.CompilerParams(vmem_limit_bytes=vmem * 2**20),
    )(*args)


def block_of(place, step):
    return lax.rem(place[3] + step, 4)


def preload_kernel(weights, tokens, weights_here, tokens_here, arrived):
    first = pltpu.make_async_copy(weights, weights_here, arrived.at[0])
    second = pltpu.make_async_copy(tokens, tokens_here, arrived.at[1])
    first.start()
    second.start()
    first.wait()
    second.wait()


def project_kernel(
    place, t0, t1, t2, t3, gain, weights, mask, normed, q_out, k_out, v_out, kv_low, kv_high, stats
):
    parts = (t0, t1, t2, t3)
    width = 4 * t0.shape[1]
    wide = [t[...].astype(F32) for t in parts]
    average = sum(jnp.sum(t, axis=1, keepdims=True) for t in wide) / width
    centered = [t - average for t in wide]
    variance = sum(jnp.sum(t * t, axis=1, keepdims=True) for t in centered) / width
    inverse_std = lax.rsqrt(variance + EPSILON)
    lane = lax.broadcasted_iota(jnp.int32, stats.shape, 1)
    stats[...] = jnp.where(lane == 0, average, inverse_std)
    for step in range(4):
        block = block_of(place, step)
        normed[block] = (centered[step] * inverse_std * gain[block]).astype(BF16)
    rows = t0.shape[1]
    for kind, out in enumerate((q_out, k_out, v_out)):
        total = None
        for block in range(4):
            term = dot_nn(normed[block], weights[kind, rows * block : rows * (block + 1), :])
            total = term if total is None else total + term
        out[...] = total.astype(BF16)
        if kind > 0:
            columns = slice((kind - 1) * rows, kind * rows)
            kv_low[:WINDOW, columns] = out[:WINDOW, :]
            kv_high[:WINDOW, columns] = out[out.shape[0] - WINDOW :, :]
    frames = t0.shape[0]
    for out, start in ((kv_low, 0), (kv_high, frames - WINDOW)):
        row = mask[:, start : start + WINDOW].astype(F32)
        out[WINDOW:, :LANES] = jnp.broadcast_to(row, (16, LANES)).astype(BF16)


def attention_kernel(
    place, mask, q_in, k_in, v_in, kv_prev, kv_next, g0, g1, g2, g3, w_out,
    attended, q_grad, kv_grad, kv_low, kv_high, gated,
    k_ext, v_ext, k_cross, v_cross, upstream, cap, dk_ext, dv_ext,
):
    frames, width = q_in.shape
    span = 3 * WINDOW
    blocks = frames // WINDOW
    turned = []
    for block in range(blocks + 2):
        if block == 0:
            row = kv_prev[WINDOW:, :LANES].astype(F32)[:1]
        elif block > blocks:
            row = kv_next[WINDOW:, :LANES].astype(F32)[:1]
        else:
            row = mask[:, (block - 1) * WINDOW : block * WINDOW].astype(F32)
        turned.append(jnp.transpose(jnp.broadcast_to(row, (WINDOW, WINDOW))))
    key_at = lax.broadcasted_iota(jnp.int32, (WINDOW, WINDOW), 0)
    query_at = lax.broadcasted_iota(jnp.int32, (WINDOW, WINDOW), 1)
    high, low = 3.0e38, -1e30
    for block in range(blocks):
        before = (key_at >= query_at) & (turned[block] > 0)
        inside = (key_at == query_at) | (turned[block + 1] > 0)
        after = (key_at <= query_at) & (turned[block + 2] > 0)
        for part, allowed in enumerate((before, inside, after)):
            cap[block, part * WINDOW : (part + 1) * WINDOW, :] = jnp.where(allowed, high, low)

    total = None
    for step, ref in enumerate((g0, g1, g2, g3)):
        block = block_of(place, step)
        for part in range(blocks):
            rows = slice(part * WINDOW, (part + 1) * WINDOW)
            keep = turned[part + 1]
            keep = jnp.concatenate([keep] * (width // WINDOW), axis=1)
            gated[block, rows, :] = (ref[rows, :].astype(F32) * keep).astype(BF16)
    for block in range(4):
        term = dot_nn(gated[block], w_out[width * block : width * (block + 1), :])
        total = term if total is None else total + term
    upstream[...] = total.astype(BF16)

    for ext, own, at in ((k_ext, k_in, 0), (v_ext, v_in, width)):
        ext[:WINDOW, :] = kv_prev[:WINDOW, at : at + width]
        ext[WINDOW : WINDOW + frames, :] = own[...]
        ext[WINDOW + frames :, :] = kv_next[:WINDOW, at : at + width]
    dk_ext[...] = jnp.zeros_like(dk_ext)
    dv_ext[...] = jnp.zeros_like(dv_ext)
    scaling = HEAD ** (-0.5)
    first = lax.broadcasted_iota(jnp.int32, (WINDOW, LANES), 1) < HEAD
    for pair in range(width // LANES):
        lanes = slice(pair * LANES, (pair + 1) * LANES)
        k_cross[...] = jnp.transpose(k_ext[:, lanes].astype(F32) * scaling).astype(BF16)
        v_cross[...] = jnp.transpose(v_ext[:, lanes].astype(F32)).astype(BF16)
        for block in range(blocks):
            rows = slice(block * WINDOW, (block + 1) * WINDOW)
            keys = slice(block * WINDOW, block * WINDOW + span)
            query = q_in[rows, lanes] * jnp.asarray(scaling, BF16)
            zero = jnp.zeros_like(query)
            query = jnp.concatenate(
                [jnp.where(first, query, zero), jnp.where(first, zero, query)], axis=0
            )
            grad = upstream[rows, lanes]
            grad = jnp.concatenate(
                [jnp.where(first, grad, zero), jnp.where(first, zero, grad)], axis=0
            )
            bound = cap[block]
            bound = jnp.concatenate([bound, bound], axis=1)
            scores = jnp.minimum(dot_nt(k_ext[keys, lanes], query), bound)
            largest = jnp.max(scores, axis=0, keepdims=True)
            exponent = jnp.exp(scores - largest)
            probability = exponent * (1.0 / jnp.sum(exponent, axis=0, keepdims=True))
            probability_low = probability.astype(BF16)
            probability_grad = dot_nt(v_ext[keys, lanes], grad)
            row_dots = jnp.sum(probability * probability_grad, axis=0, keepdims=True)
            score_grad = (probability * (probability_grad - row_dots)).astype(BF16)
            dv_ext[keys, lanes] += dot_nn(probability_low, grad)
            dk_ext[keys, lanes] += dot_nn(score_grad, query)
            for cross, factor, out in (
                (v_cross, probability_low, attended),
                (k_cross, score_grad, q_grad),
            ):
                both = dot_nn(cross[:, keys], factor)
                both = jnp.concatenate([both[:HEAD, :WINDOW], both[HEAD:, WINDOW:]], axis=0)
                out[rows, lanes] = jnp.transpose(both).astype(BF16)
    for ext, at in ((dk_ext, 0), (dv_ext, width)):
        columns = slice(at, at + width)
        kv_low[:, columns] = ext[:WINDOW, :].astype(BF16)
        kv_grad[:, columns] = ext[WINDOW : WINDOW + frames, :]
        kv_high[:, columns] = ext[WINDOW + frames :, :].astype(BF16)


def split_rows(place, block, held, send, keep):
    core = place[2]
    for group in range(8):
        at = group % 4 * 8 + 2 * block + group // 4
        for out, whose in ((send, 1 - core), (keep, core)):
            start = pl.multiple_of(48 * group + 24 * whose, 8)
            both = jnp.concatenate([held[0, pl.ds(start, 24), :], held[1, pl.ds(start, 24), :]], 0)
            out[at] = both.astype(BF16)


def folded(value):
    return value[:, :LANES] + value[:, LANES : 2 * LANES] + value[:, 2 * LANES :]


def in_two(value):
    head = value.astype(BF16).astype(F32)
    return jnp.concatenate([head, value - head], axis=0).astype(BF16)


def from_two(value):
    wide = value.astype(F32)
    return wide[:8] + wide[8:16]


def first_weights_kernel(
    place, gated, attended, q_grad, normed, weights, send, keep, gain_sums, held
):
    width = attended.shape[1]
    for block in range(4):
        rows = slice(width * block, width * (block + 1))
        held[0] = dot_tn(gated[block], attended[...])
        held[1] = dot_tn(normed[block], q_grad[...])
        gain_sums[block] = folded(held[1] * weights[0, rows, :].astype(F32))
        split_rows(place, block, held, send, keep)


def branch_kernel(attended, w_out, branches):
    width = attended.shape[1]
    for block in range(4):
        rows = w_out[width * block : width * (block + 1), :]
        branches[block] = dot_nt(attended[...], rows).astype(BF16)


def second_weights_kernel(
    place, kv_grad, from_prev, from_next, normed, weights, gain_sums, gain,
    send, keep, k_grad, v_grad, gain_part, held,
):
    frames, width = k_grad.shape
    for out, at in ((k_grad, 0), (v_grad, width)):
        columns = slice(at, at + width)
        out[:WINDOW, :] = (
            kv_grad[:WINDOW, columns] + from_prev[:, columns].astype(F32)
        ).astype(BF16)
        out[WINDOW : frames - WINDOW, :] = kv_grad[WINDOW : frames - WINDOW, columns].astype(BF16)
        out[frames - WINDOW :, :] = (
            kv_grad[frames - WINDOW :, columns] + from_next[:, columns].astype(F32)
        ).astype(BF16)
    gain_part[...] = jnp.zeros_like(gain_part)
    for block in range(4):
        rows = slice(width * block, width * (block + 1))
        held[0] = dot_tn(normed[block], k_grad[...])
        held[1] = dot_tn(normed[block], v_grad[...])
        sums = gain_sums[block] + folded(
            held[0] * weights[1, rows, :].astype(F32) + held[1] * weights[2, rows, :].astype(F32)
        )
        for part in range(width // LANES):
            lanes = slice(part * LANES, (part + 1) * LANES)
            turned = jnp.transpose(sums[lanes, :])
            row = jnp.sum(turned, axis=0, keepdims=True)
            gain_part[block : block + 1, lanes] = row / gain[block][:, lanes]
        split_rows(place, block, held, send, keep)
    send[32, :16, :] = in_two(gain_part[...])


def norm_kernel(
    place, branches, q_grad, k_grad, v_grad, weights, normed, gain, n0, n1, n2, n3
):
    frames, width = q_grad.shape
    first_sum = second_sum = None
    for step, out in enumerate((n0, n1, n2, n3)):
        block = block_of(place, step)
        rows = pl.ds(pl.multiple_of(width * block, width), width)
        total = None
        for kind, part in enumerate((q_grad, k_grad, v_grad)):
            term = dot_nt(part[...], weights[kind, rows, :])
            total = term if total is None else total + term
        out[:frames, :] = total.astype(BF16)
        out[frames + 16 :, :] = branches[block]
        first = jnp.sum(total * gain[block], axis=1, keepdims=True)
        second = jnp.sum(total * normed[block].astype(F32), axis=1, keepdims=True)
        first_sum = first if first_sum is None else first_sum + first
        second_sum = second if second_sum is None else second_sum + second
    lane = lax.broadcasted_iota(jnp.int32, (frames, LANES), 1)
    sums = jnp.transpose(jnp.where(lane == 0, first_sum, jnp.where(lane == 1, second_sum, 0.0)))
    tail = in_two(sums[:8, :])
    for out in (n0, n1, n2, n3):
        out[frames : frames + 16, :] = tail


def tokens_kernel(place, gain, tokens, out_grad, stats, n0, n1, n2, n3, out):
    frames = tokens.shape[0]
    width = 4 * tokens.shape[1]
    average, inverse_std = stats[:, 0:1], stats[:, 1:2]
    total, rows = None, None
    for ref in (n0, n1, n2, n3):
        part = ref[:frames, :].astype(F32)
        tail = from_two(ref[frames : frames + 16, :])
        total = part if total is None else total + part
        rows = tail if rows is None else rows + tail
    rows = jnp.concatenate([rows, jnp.zeros((LANES - 8, frames), F32)], axis=0) / width
    turned = jnp.transpose(rows)
    first_mean, second_mean = turned[:, 0:1], turned[:, 1:2]
    whitened = (tokens[...].astype(F32) - average) * inverse_std
    unit = total * gain[place[3]]
    moved = (unit - first_mean - whitened * second_mean) * inverse_std
    out[...] = (out_grad[...].astype(F32) + moved).astype(BF16)


def layer_kernel(tokens, mask, n0, n1, n2, n3, out):
    total = None
    for ref in (n0, n1, n2, n3):
        term = ref[tokens.shape[0] + 16 :, :].astype(F32)
        total = term if total is None else total + term
    for part in range(tokens.shape[0] // WINDOW):
        rows = slice(part * WINDOW, (part + 1) * WINDOW)
        row = mask[:, rows].astype(F32)
        keep = jnp.transpose(jnp.broadcast_to(row, (WINDOW, WINDOW)))
        keep = jnp.concatenate([keep] * (tokens.shape[1] // WINDOW), axis=1)
        out[rows, :] = (tokens[rows, :].astype(F32) + keep * total[rows, :]).astype(BF16)


def core_sum(place, keep, received, send, own):
    parity = lax.rem(place[0], 2)
    for out, whose in ((send, 1 - parity), (own, parity)):
        for x in range(4):
            for far in range(4):
                which = 8 * x + 2 * far + whose
                total = keep[which].astype(F32) + received[which].astype(F32)
                out[4 * x + far] = total.astype(out.dtype)


def first_core_kernel(place, keep, received, send, own):
    core_sum(place, keep, received, send, own)


def gain_kernel(received, gain_part, gain_sum):
    gain_sum[...] = from_two(in_two(gain_part[...])) + from_two(received[32, :16, :])


def second_core_kernel(place, keep, received, g0, g1, g2, g3, send, own, gain_sum):
    core_sum(place, keep, received, send, own)
    gain_sum[...] = (g0[...] + g2[...]) + (g1[...] + g3[...])
    send[16, :16, :] = in_two(gain_sum[...])


def first_near_kernel(keep, received, total):
    for which in range(16):
        total[which] = keep[which] + received[which].astype(F32)


def near_kernel(place, sum1, keep, received, gain_part, own, p1, p2, p3, gain_sum):
    gain_sum[...] = from_two(in_two(gain_part[...])) + from_two(received[16, :16, :])
    for step, out in enumerate((own, p1, p2, p3)):
        for far in range(4):
            which = lax.rem(place[1] + step, 4) * 4 + far
            out[96 * far : 96 * far + 48, :] = sum1[which].astype(out.dtype)
            total = keep[which] + received[which].astype(F32)
            out[96 * far + 48 : 96 * far + 96, :] = total.astype(out.dtype)
        if step:
            out[384:, :] = in_two(gain_sum[...])


def x_sum_kernel(place, kept, r1, r2, r3, gain_part, own, p1, p2, p3, gain_sum):
    near = from_two(in_two(gain_part[...])) + from_two(r2[384:, :])
    gain_sum[...] = near + (from_two(r1[384:, :]) + from_two(r3[384:, :]))
    for step, out in enumerate((own, p1, p2, p3)):
        far = lax.rem(lax.div(place[0], 2) + step, 4)
        rows = pl.ds(pl.multiple_of(96 * far, 32), 96)
        total = kept[rows, :] + r2[rows, :].astype(F32)
        total = total + (r1[rows, :].astype(F32) + r3[rows, :].astype(F32))
        out[:96, :] = total.astype(out.dtype)
        if step:
            out[96:, :] = in_two(gain_sum[...])


def far_sum_kernel(own, r1, r2, r3, gain_part, out_weight, qkv_weight, gain_sum):
    total = own[...] + r2[:96, :].astype(F32)
    total = total + (r1[:96, :].astype(F32) + r3[:96, :].astype(F32))
    out_weight[...] = total[:24]
    for kind in range(3):
        qkv_weight[kind] = total[24 * (kind + 1) : 24 * (kind + 2)]
    near = from_two(in_two(gain_part[...])) + from_two(r2[96:, :])
    total = near + (from_two(r1[96:, :]) + from_two(r3[96:, :]))
    width = total.shape[1]
    for block in range(4):
        gain_sum[:, width * block : width * (block + 1)] = total[block : block + 1, :]


def per_device(tokens, ln_gain, w_qkv, w_out, frame_mask, out_grad):
    frames, width = tokens.shape
    place = jnp.stack([lax.axis_index(a) for a in ("z", "x", "core", "tp")]).astype(jnp.int32)
    token_parts = [tokens] + [shifted(tokens, "tp", -step) for step in (1, 2, 3)]
    late, token_parts[3] = lax.optimization_barrier((out_grad, token_parts[3]))
    grad_parts = [out_grad] + [shifted(late, "tp", -step) for step in (1, 2, 3)]
    mask_row = frame_mask[None, :]
    gain = ln_gain.reshape(4, 1, width)
    weights = jnp.transpose(w_qkv, (1, 0, 2))
    weights_here, token_parts[0] = call(
        preload_kernel,
        [(weights.shape, BF16), ((frames, width), BF16)],
        (weights, tokens),
        far=(0, 1),
        scratch=[pltpu.SemaphoreType.DMA((2,))],
        cost=2**30,
        vmem=8,
    )

    sheet, wide_sheet = ((frames, width), BF16), ((4, frames, width), BF16)
    edge, halo = ((WINDOW, 2 * width), BF16), ((WINDOW + 16, 2 * width), BF16)
    square = frames * width * width * 2
    normed, q_own, k_own, v_own, kv_low, kv_high, stats = call(
        project_kernel,
        [wide_sheet, sheet, sheet, sheet, halo, halo, ((frames, LANES), F32)],
        (place, *token_parts, gain, weights_here, mask_row),
        smem=(0,),
        cost=12 * square,
    )
    kv_prev, kv_next = to_next(kv_high), to_previous(kv_low)
    span = frames + 2 * WINDOW
    attended, q_grad, kv_grad, edge_low, edge_high, gated = call(
        attention_kernel,
        [sheet, sheet, ((frames, 2 * width), F32), edge, edge, wide_sheet],
        (place, mask_row, q_own, k_own, v_own, kv_prev, kv_next, *grad_parts, w_out),
        smem=(0,),
        scratch=[
            pltpu.VMEM((span, width), BF16),
            pltpu.VMEM((span, width), BF16),
            pltpu.VMEM((LANES, span), BF16),
            pltpu.VMEM((LANES, span), BF16),
            pltpu.VMEM((frames, width), BF16),
            pltpu.VMEM((frames // WINDOW, 3 * WINDOW, WINDOW), F32),
            pltpu.VMEM((span, width), F32),
            pltpu.VMEM((span, width), F32),
        ],
    )
    from_next, from_prev = to_previous(edge_low), to_next(edge_high)
    held = pltpu.VMEM((2, frames, width), F32)

    def pieces(count, dtype=BF16):
        return ((count, 48, width), dtype)

    small = ((8, width), F32)
    send, keep, gain_sums = call(
        first_weights_kernel,
        [pieces(32), pieces(32), ((4, frames, LANES), F32)],
        (place, gated, attended, q_grad, normed, weights),
        smem=(0,),
        scratch=[held],
        cost=12 * square,
    )
    received = swapped(send, "core", 1)
    (branches,) = call(branch_kernel, [wide_sheet], (attended, w_out), cost=4 * square)
    branches, from_prev, from_next, received = lax.optimization_barrier(
        (branches, from_prev, from_next, received)
    )
    send2, keep2, k_grad, v_grad, gain_part = call(
        second_weights_kernel,
        [pieces(33), pieces(32), sheet, sheet, small],
        (place, kv_grad, from_prev, from_next, normed, weights, gain_sums, gain),
        smem=(0,),
        scratch=[held],
    )
    received2 = swapped(send2, "core", 1)
    near1, keep1 = call(
        first_core_kernel,
        [pieces(16), pieces(16, F32)],
        (place, keep, received),
        smem=(0,),
        vmem=16,
    )
    k_grad, near1 = lax.optimization_barrier((k_grad, near1))
    near1 = swapped(near1, "z", 1)
    exchanged = call(
        norm_kernel,
        [((2 * frames + 16, width), BF16)] * 4,
        (place, branches, q_grad, k_grad, v_grad, weights, normed, gain),
        smem=(0,),
    )
    exchanged = list(exchanged)
    received2, exchanged[0] = lax.optimization_barrier((received2, exchanged[0]))
    (gain_part,) = call(gain_kernel, [small], (received2, gain_part), vmem=8)
    gains = [gain_part] + [shifted(gain_part, "tp", by) for by in (1, 2, 3)]
    near2, keep2, gain_part = call(
        second_core_kernel,
        [pieces(17), pieces(16, F32), small],
        (place, keep2, received2, *gains),
        smem=(0,),
        vmem=16,
    )
    near2 = across(near2, "z")
    (sum1,) = call(first_near_kernel, [pieces(16, F32)], (keep1, near1), vmem=16)
    exchanged, gain_part = lax.optimization_barrier((exchanged, gain_part))
    exchanged = list(exchanged)
    exchanged[1:] = [shifted(part, "tp", by + 1) for by, part in enumerate(exchanged[1:])]
    own, *parts, gain_part = call(
        near_kernel,
        [((384, width), F32)] + [((400, width), BF16)] * 3 + [small],
        (place, sum1, keep2, near2, gain_part),
        smem=(0,),
        vmem=16,
    )
    received = [shifted(part, "x", by + 1) for by, part in enumerate(parts)]
    received[2], exchanged[1] = lax.optimization_barrier((received[2], exchanged[1]))
    own, *parts, gain_part = call(
        x_sum_kernel,
        [((96, width), F32)] + [((112, width), BF16)] * 3 + [small],
        (place, own, *received, gain_part),
        smem=(0,),
        vmem=16,
    )
    received = [shifted(part, "z", 2 * (by + 1)) for by, part in enumerate(parts)]
    (layer_out,) = call(layer_kernel, [sheet], (tokens, mask_row, *exchanged), vmem=16)
    (tokens_grad,) = call(
        tokens_kernel,
        [sheet],
        (place, gain, tokens, out_grad, stats, *exchanged),
        smem=(0,),
        vmem=16,
    )
    received[2], layer_out, tokens_grad = lax.optimization_barrier(
        (received[2], layer_out, tokens_grad)
    )
    out_weight_grad, qkv_grad, gain_grad = call(
        far_sum_kernel,
        [((24, width), F32), ((3, 24, width), F32), ((1, 4 * width), F32)],
        (own, *received, gain_part),
        vmem=16,
    )
    return (
        layer_out,
        tokens_grad,
        gain_grad.reshape(-1),
        jnp.transpose(qkv_grad, (1, 0, 2)),
        out_weight_grad,
    )


def solution(mesh):
    split = Mesh(mesh.devices.reshape(8, 4, 2, 4), ("z", "x", "core", "tp"))
    return jax.shard_map(
        per_device,
        mesh=split,
        in_specs=(P(TM, "tp"), P(), P(None, None, "tp"), P(None, "tp"), P(TM), P(TM, "tp")),
        out_specs=(P(TM, "tp"), P(TM, "tp"), P(), P(TM, None, "tp"), P(TM, "tp")),
        check_vma=False,
    )
```
